128 devices in a mesh: store: 8 (over x, core), ep: 16 (over y, z).
Axes of the slice: x: 4, y: 4, z: 4, core: 2. Of those that a mesh axis runs over, the one named last changes fastest.
Arguments:
- queries: bfloat16 [1024, 36864], P('store', 'ep'), may hold values from -30 to 30
- residual_in: bfloat16 [1024, 7168], P(('store', 'ep')), may hold values from -6 to 6
- latent_store: bfloat16 [256, 128, 576], P('store'), may hold values from -5 to 5
- group_passages: int32 [256], replicated, may hold values from 0 to 255, as said below
- row_slots: int32 [1024, 16], P('store'), may hold values from 0 to 31, as said below
- passage_place: int32 [256], replicated, may hold values from 0 to 255, as said below
- w_uv: bfloat16 [64, 512, 128], P('ep'), may hold values from -0.25 to 0.25
- w_out: bfloat16 [8192, 7168], P('ep'), may hold values from -0.5 to 0.5
- expert_ids: int32 [1024, 4], P(('store', 'ep')), may hold values from 0 to 15, all different within a row; in each aligned block of 8 rows (0 to 7, 8 to 15, ...) at most 4 rows name the same one
- expert_gates: float32 [1024, 4], P(('store', 'ep')), may hold values from 0.2 to 1.2
- w_gate: bfloat16 [16, 7168, 2048], P('ep', None, 'store'), may hold values from -0.0625 to 0.0625
- w_up: bfloat16 [16, 7168, 2048], P('ep', None, 'store'), may hold values from -0.0625 to 0.0625
- w_down: bfloat16 [16, 2048, 7168], P('ep', 'store'), may hold values from -0.125 to 0.125
Outputs:
- layer_out: bfloat16 [1024, 7168], P(('store', 'ep'))
The draws below stay inside these ranges and needn't reach their ends.
Inputs may be any that keep to these rules, and one draw needn't show every extreme that they name: A permutation: passage p lies in row passage_place[p] of latent_store. `group_passages`: the 32 passages of one group are distinct, and slot i of every group's list names a passage held by store shard i // 4, that is with passage_place in [(i // 4) * 32, (i // 4 + 1) * 32). `row_slots`: each row names 16 distinct slots. `expert_ids`: each row names 4 different experts; among the rows of one device no expert is named by more than 4 rows.
All inputs are finite; a program needn't handle non-finite values.
Results may differ from the reference program's by a relative error of at most 0.022.
Values may be sent and summed in bfloat16 or wider, within the bound.
A program may use at most 128 MiB of HBM per device.

```python
import math
import jax
import jax.numpy as jnp
import numpy as np
from jax import lax

D = 7168
LAT = 512
HEADS = 64
HEAD_V = 128
MOE_FF = 2048
PSG_LEN = 128
TOP = 4
CAP_P = 4
NP_SHARD = 32
TOK_DEV = 8
QK = 576
GRP_ROWS = 128
ROWS = 1024
SLOTS = 32
PSG = 16
PASSAGES = 256
CAP_X = 4
N_STORE = 8
N_EP = 16


def passage_tables(key):
    key = jax.random.fold_in(key, 11)
    first_key, second_key = jax.random.split(key)
    store_rows = jax.random.permutation(first_key, PASSAGES).astype(jnp.int32)
    owner_ids = jnp.argsort(store_rows).astype(jnp.int32)
    position = jnp.arange(NP_SHARD, dtype=jnp.int32)
    random_ranks = jax.random.randint(second_key, (N_STORE, N_STORE, NP_SHARD), 0, 1 << 20) * NP_SHARD + position
    local_rows = jnp.argsort(random_ranks, axis=2)[:, :, :CAP_P].astype(jnp.int32)
    shard_base = (jnp.arange(N_STORE, dtype=jnp.int32) * NP_SHARD)[None, :, None]
    passage_ids = owner_ids[shard_base + local_rows].reshape(N_STORE * SLOTS)
    return (store_rows, passage_ids)


def row_choice(key):
    key = jax.random.fold_in(key, 13)
    position = jnp.arange(SLOTS, dtype=jnp.int32)
    random_ranks = jax.random.randint(key, (ROWS, SLOTS), 0, 1 << 20) * SLOTS + position
    return jnp.argsort(random_ranks, axis=1)[:, :PSG].astype(jnp.int32)


def latent_values(key):
    key = jax.random.fold_in(key, 17)
    first_key = jax.random.fold_in(key, 0)
    base = jax.random.truncated_normal(first_key, -4.0, 4.0, (PASSAGES, PSG_LEN, QK), jnp.float32)
    second_token = base[:, 1]
    return base.at[:, 1].set(second_token)


def draw_passage_place(key, part):
    return passage_tables(key)[0]


def draw_group_passages(key, part):
    return passage_tables(key)[1]


def draw_row_slots(key, part):
    return row_choice(key)


def draw_latent_store(key, part):
    values = latent_values(key)
    return values.astype(jnp.bfloat16)


def draw_queries(key, part):
    key = jax.random.fold_in(key, 19)
    drawn = jax.random.truncated_normal(key, -4.0, 4.0, (ROWS, HEADS, QK), jnp.float32)
    return drawn.reshape(ROWS, HEADS * QK).astype(jnp.bfloat16)


def levels(own_key, shape, cuts, smallest, high):
    level, own = 1.0, jax.random.fold_in(own_key, 6)
    for dim, blocks in cuts:
        heights = jnp.exp(jax.random.uniform(jax.random.fold_in(own, dim), (blocks,), jnp.float32, smallest / len(cuts), high / len(cuts)))
        level = level * jnp.repeat(heights, shape[dim] // blocks).reshape([-1 if axis == dim else 1 for axis in range(len(shape))])
    return level


def deal_out(stream_key, own, number, rows, amount, top, limit, skew):
    order = jax.random.permutation(stream_key, amount)
    crowded, usual = shares(amount, rows * top, limit, skew, True), shares(amount, rows * top, limit, skew, False)
    places = jnp.arange(amount)

    def named(lengths, offset_by):
        used = int((lengths > 0).sum())
        fixed = max(1, used // 4)
        passed = fixed + (places - fixed + offset_by * (used - fixed)) % max(1, amount - fixed)
        return jnp.zeros((amount,), jnp.int32).at[order[jnp.where(places < fixed, places, passed)]].set(jnp.asarray(lengths, jnp.int32))

    lengths = jnp.where(number % 4 == 0, named(crowded, number // 4), named(usual, number - number // 4 - 1))
    mixed = jax.random.permutation(jax.random.fold_in(own, 3), amount)
    giver, sink = mixed[0:amount // 2 * 2:2], mixed[1:amount // 2 * 2:2]
    slack = jnp.minimum(lengths[giver] - 1, limit - lengths[sink]) // 2
    slack = jnp.where((giver == order[0]) | (sink == order[0]) | (lengths[sink] == 0), 0, jnp.maximum(slack, 0))
    passed = jax.random.randint(jax.random.fold_in(own, 4), (amount // 2,), 0, 1 << 20) % (slack + 1)
    lengths = lengths.at[giver].add(-passed).at[sink].add(passed)
    members = jnp.searchsorted(jnp.cumsum(lengths), jnp.arange(rows * top), side="right").astype(jnp.int32)
    table = members.reshape(top, rows).T
    table = table[jax.random.permutation(jax.random.fold_in(own, 1), rows)]
    offset_by = jax.random.randint(jax.random.fold_in(own, 2), (rows, 1), 0, top)
    return jnp.take_along_axis(table, (jnp.arange(top)[None, :] + offset_by) % top, axis=1)


def shares(amount, total, most, skew, full):
    loads = [(1 << 20) // math.isqrt(rank ** skew) + 1 for rank in range(1, amount + 1)]
    largest = most if full else min(most, max(-(-total // amount), total * loads[0] // sum(loads)))
    least = 1 if total - largest >= amount - 1 else 0
    holding, rest = [largest] + [least] * (amount - 1), total - largest - least * (amount - 1)
    while rest > 0:
        movable = [i for i in range(1, amount) if holding[i] < largest] or [i for i in range(1, amount) if holding[i] < most]
        mass, remaining = sum([loads[i] for i in movable]), rest
        for i in movable:
            addition = min(most - holding[i], max(1, remaining * loads[i] // mass), rest)
            holding[i] = holding[i] + addition
            rest = rest - addition
    return np.array(holding)


def centred(rng, shape, deviation, bound, shards=(), held_as=jnp.bfloat16):
    values = deviation * jax.random.normal(rng, shape, jnp.float32)
    if shards:
        values = values * levels(rng, shape, shards, -0.22, 0.18)
    return jnp.clip(values, -bound, bound).astype(held_as)


def setup_inputs(seed: int = 0) -> dict:
    keys = jax.random.split(jax.random.key(seed), 14)
    queries = draw_queries(jax.random.fold_in(keys[13], 71), 0)
    residual_in = centred(keys[1], (ROWS, D), 1.0, 6.0, ((0, 128),))
    latent_store = draw_latent_store(jax.random.fold_in(keys[13], 71), 0)
    group_passages = draw_group_passages(jax.random.fold_in(keys[13], 71), 0)
    row_slots = draw_row_slots(jax.random.fold_in(keys[13], 71), 0)
    passage_place = draw_passage_place(jax.random.fold_in(keys[13], 71), 0)
    w_uv = centred(keys[6], (HEADS, LAT, HEAD_V), LAT ** -0.5, 0.25, ((0, 16),))
    w_out = centred(keys[7], (HEADS * HEAD_V, D), HEAD_V ** -0.5, 0.5, ((0, 16),))
    expert_ids_keys = jax.random.split(jax.random.fold_in(keys[8], 1), ROWS // TOK_DEV)
    expert_ids_turns = jax.random.permutation(jax.random.fold_in(keys[8], 3), ROWS // TOK_DEV)
    expert_ids = jax.vmap(lambda own, number: deal_out(jax.random.fold_in(keys[8], 2), own, number, TOK_DEV, N_EP, TOP, CAP_X, 2))(expert_ids_keys, expert_ids_turns).reshape((ROWS, TOP))
    expert_gates = jnp.clip(0.2 + 1 * jax.random.uniform(keys[9], (ROWS, TOP), jnp.float32) ** levels(keys[9], (ROWS, TOP), ((0, 128),), -0.2, 0.2), 0.2, 1.2)
    w_gate = centred(keys[10], (N_EP, D, MOE_FF), D ** -0.5, 0.0625, ((0, 16), (2, 8)))
    w_up = centred(keys[11], (N_EP, D, MOE_FF), D ** -0.5, 0.0625, ((0, 16), (2, 8)))
    w_down = centred(keys[12], (N_EP, MOE_FF, D), MOE_FF ** -0.5, 0.125, ((0, 16), (1, 8)))
    return {"queries": queries, "residual_in": residual_in, "latent_store": latent_store, "group_passages": group_passages, "row_slots": row_slots, "passage_place": passage_place, "w_uv": w_uv, "w_out": w_out, "expert_ids": expert_ids, "expert_gates": expert_gates, "w_gate": w_gate, "w_up": w_up, "w_down": w_down}


score_scale = 192.0 ** (-0.5)

def attend_group(inputs, latent_store, w_uv, w_out):
    query_rows, store_rows, chosen_slots = inputs
    key_rows = latent_store[store_rows].reshape(SLOTS * PSG_LEN, QK).astype(jnp.float32)
    slot_range = jnp.arange(SLOTS, dtype=jnp.int32)
    chosen = jnp.any(chosen_slots[:, :, None] == slot_range[None, None, :], axis=1)
    kept_mask = jnp.repeat(chosen, PSG_LEN, axis=1)[:, None, :]
    scores = jnp.einsum('rhc,tc->rht', query_rows.astype(jnp.float32), key_rows, precision=lax.Precision.HIGHEST) * score_scale
    row_max = lax.optimization_barrier(jnp.max(jnp.where(kept_mask, scores, -jnp.inf), axis=2, keepdims=True))
    exponent = jnp.where(kept_mask, jnp.exp(scores - row_max), 0.0)
    weights = (exponent / lax.optimization_barrier(jnp.sum(exponent, axis=2, keepdims=True))).astype(jnp.bfloat16)
    latent_out = jnp.einsum('rht,tc->rhc', weights.astype(jnp.float32), key_rows[:, :LAT], precision=lax.Precision.HIGHEST).astype(jnp.bfloat16)
    head_out = jnp.einsum('rhc,hcv->rhv', latent_out.astype(jnp.float32), w_uv.astype(jnp.float32), precision=lax.Precision.HIGHEST).astype(jnp.bfloat16)
    return jnp.dot(head_out.reshape(GRP_ROWS, HEADS * HEAD_V), w_out, preferred_element_type=jnp.float32)

def reference(queries, residual_in, latent_store, group_passages, row_slots, passage_place, w_uv, w_out, expert_ids, expert_gates, w_gate, w_up, w_down):
    store_rows = passage_place[group_passages].astype(jnp.int32).reshape(N_STORE, SLOTS)
    query_groups = queries.reshape(N_STORE, GRP_ROWS, HEADS, QK)
    slot_groups = row_slots.reshape(N_STORE, GRP_ROWS, PSG)
    attended = lax.map(lambda inputs: attend_group(inputs, latent_store, w_uv, w_out), (query_groups, store_rows, slot_groups))
    mixed_rows = residual_in.astype(jnp.float32) + attended.reshape(ROWS, D)
    normed = (mixed_rows * lax.rsqrt(lax.optimization_barrier(jnp.mean(mixed_rows * mixed_rows, axis=1, keepdims=True)) + 1e-06)).astype(jnp.bfloat16)
    flat_ids = expert_ids.reshape(ROWS * TOP).astype(jnp.int32)
    flat_gates = expert_gates.reshape(ROWS * TOP)
    pair_bound = ROWS // TOK_DEV * CAP_X

    def add_expert(running, expert):
        matches = flat_ids == expert
        picked = jnp.nonzero(matches, size=pair_bound, fill_value=0)[0].astype(jnp.int32)
        live_pairs = jnp.arange(pair_bound, dtype=jnp.int32) < jnp.sum(matches.astype(jnp.int32))
        row_index = picked // TOP
        row_block = normed[row_index]
        gate_proj = jnp.dot(row_block, w_gate[expert], preferred_element_type=jnp.float32)
        up_proj = jnp.dot(row_block, w_up[expert], preferred_element_type=jnp.float32)
        hidden = (jax.nn.silu(gate_proj) * up_proj).astype(jnp.bfloat16)
        partials = jnp.einsum('nsf,sfd->nsd', hidden.reshape(pair_bound, N_STORE, MOE_FF // N_STORE).astype(jnp.float32), w_down[expert].reshape(N_STORE, MOE_FF // N_STORE, D).astype(jnp.float32), precision=lax.Precision.HIGHEST)
        rounded = lax.optimization_barrier(partials.astype(jnp.bfloat16))
        expert_rows = lax.optimization_barrier(jnp.sum(rounded.astype(jnp.float32), axis=1)).astype(jnp.bfloat16)
        pair_gates = jnp.where(live_pairs, flat_gates[picked], 0.0)
        return (running.at[row_index].add(pair_gates[:, None] * expert_rows.astype(jnp.float32)), None)
    expert_mix = lax.scan(add_expert, jnp.zeros((ROWS, D), jnp.float32), jnp.arange(N_EP, dtype=jnp.int32))[0]
    return (mixed_rows + expert_mix).astype(jnp.bfloat16)
```

```python
import functools

import jax
import jax.numpy as jnp
from jax import lax
from jax.experimental import pallas as pl
from jax.experimental.pallas import tpu as pltpu
from jax.sharding import PartitionSpec as P

score_scale = 192.0 ** (-0.5)
MESH = pl.DeviceIdType.MESH
LOW = -1e30


def offset_of(i):
    return i + i // 2 - 2 * (i // 3)


def attend_kernel(
    served, queries, chosen, w_uv, w_out, residual, w_down,
    mixed, normed, down_cols,
    kv, heads, mask, top, total, acc, head_out, out_w, part, part_in, summed, summed_in, rows,
    x_send, x_recv, g_send, g_recv, r_send, r_recv, d_send, d_recv, w_sem,
):
    s = lax.axis_index("store")
    e = lax.axis_index("ep")
    y, z = e // 4, e % 4

    def at_y(d):
        return (s, lax.rem(y + d, 4) * 4 + z)

    def at_z(d):
        return (s, y * 4 + lax.rem(z + d, 4))

    def at_s(d):
        return (lax.rem(s + d, 8), e)

    peers = [at_s(d) for d in range(1, 8)] + [at_y(d) for d in (1, 2, 3)] + [at_z(d) for d in (1, 2, 3)]
    barrier = pltpu.get_barrier_semaphore()
    for peer in peers:
        pl.semaphore_signal(barrier, inc=1, device_id=peer, device_id_type=MESH)
    get_w = pltpu.make_async_copy(w_out, out_w, w_sem.at[0])
    get_w.start()
    pl.semaphore_wait(barrier, len(peers))

    sent = []
    for d in range(1, 8):
        to = at_s(d)
        copy = pltpu.make_async_remote_copy(
            src_ref=served.at[to[0]],
            dst_ref=kv.at[e, pl.ds(pl.multiple_of(s * 32, 32), 32)],
            send_sem=x_send.at[d - 1], recv_sem=x_recv.at[d - 1],
            device_id=to, device_id_type=MESH,
        )
        copy.start()
        sent.append(copy)
    kv[e, pl.ds(pl.multiple_of(s * 32, 32), 32)] = served[s]

    for h in range(4):
        heads[h] = queries[:, h * 576:(h + 1) * 576]
    slot_row = lax.broadcasted_iota(jnp.int32, (32, 256), 0)
    token_col = lax.broadcasted_iota(jnp.int32, (32, 256), 1)
    for j in range(4):
        spread = (slot_row == (token_col // 32) * 4 + j).astype(jnp.bfloat16)
        mask[j] = jnp.dot(chosen[...], spread, preferred_element_type=jnp.float32)
    top[...] = jnp.full_like(top, LOW)
    total[...] = jnp.zeros_like(total)
    acc[...] = jnp.zeros_like(acc)

    def chunk(half, first, second):
        dy, dz = (first, second) if half == 0 else (second, first)
        return lax.rem(y - dy + 4, 4) * 4 + lax.rem(z - dz + 4, 4)

    def attend(p_a, p_b):
        keys = jnp.concatenate([kv[p_a, 0:128], kv[p_b, 128:256]], axis=0)
        live = jnp.concatenate([mask[p_a // 4][:, 0:128], mask[p_b // 4][:, 128:256]], axis=1)
        for h in range(4):
            scores = lax.dot_general(
                heads[h], keys, (((1,), (1,)), ((), ())), preferred_element_type=jnp.float32
            ) * score_scale
            scores = jnp.where(live > 0.5, scores, LOW)
            old = top[h]
            new = jnp.maximum(old, jnp.max(scores, axis=1, keepdims=True))
            exponent = jnp.exp(scores - new[:, 0:1]) * live
            scale = jnp.exp(old - new)
            top[h] = new
            total[h] = total[h] * scale + jnp.sum(exponent, axis=1, keepdims=True)
            acc[h] = acc[h] * scale[:, 0:1] + jnp.dot(
                exponent.astype(jnp.bfloat16), keys[:, 0:512], preferred_element_type=jnp.float32
            )

    def gather_copy(half, group, kind, place):
        low = half * 128 + (64 if kind == 3 else 0)
        size = 64 if kind >= 2 else 128
        on_y = (half == 0) == (group is None)
        to = (at_y if on_y else at_z)(1 if kind % 2 == 0 else 3)
        block = kv.at[place, pl.ds(low, size)]
        index = 4 if group is None else group
        return pltpu.make_async_remote_copy(
            src_ref=block, dst_ref=block,
            send_sem=g_send.at[half, index, kind], recv_sem=g_recv.at[half, index, kind],
            device_id=to, device_id_type=MESH,
        )

    def launch(group, offset):
        for half in (0, 1):
            for kind in (0, 1):
                gather_copy(half, group, kind, chunk(half, offset, 0)).start()

    for copy in sent:
        copy.wait_recv()
    launch(None, 0)
    launch(0, 0)
    attend(e, e)
    for kind in (0, 1):
        offset = 1 if kind == 0 else 3
        for half in (0, 1):
            gather_copy(half, None, kind, e).wait_recv()
            gather_copy(half, None, kind + 2, chunk(half, offset, 0)).start()
        launch(kind + 1, offset)

    def near(i, _):
        offset = 1 + 2 * i
        attend(chunk(0, offset, 0), chunk(1, offset, 0))
        return 0

    lax.fori_loop(0, 2, near, 0)
    for half in (0, 1):
        for kind in (2, 3):
            gather_copy(half, None, kind, e).wait_recv()
    launch(3, 2)
    attend(chunk(0, 2, 0), chunk(1, 2, 0))

    def sides(i, _):
        offset = offset_of(i)
        for kind in (0, 1):
            back = 1 if kind == 0 else 3
            for half in (0, 1):
                gather_copy(half, i, kind, e).wait_recv()
                gather_copy(half, i, kind + 2, chunk(half, offset, back)).start()

        def both(k, _):
            attend(chunk(0, offset, 1 + 2 * k), chunk(1, offset, 1 + 2 * k))
            return 0

        lax.fori_loop(0, 2, both, 0)
        return 0

    lax.fori_loop(0, 4, sides, 0)

    def far(i, _):
        offset = offset_of(i)
        for half in (0, 1):
            for kind in (2, 3):
                gather_copy(half, i, kind, e).wait_recv()
        attend(chunk(0, offset, 2), chunk(1, offset, 2))
        return 0

    lax.fori_loop(0, 4, far, 0)

    for h in range(4):
        latent = (acc[h] / total[h][:, 0:1]).astype(jnp.bfloat16)
        head_out[:, h * 128:(h + 1) * 128] = jnp.dot(
            latent, w_uv[h], preferred_element_type=jnp.float32
        ).astype(jnp.bfloat16)
    get_w.wait()

    first = []
    for half in (0, 1):
        def project(t, _):
            lane = pl.multiple_of(t * 256, 256)
            both = []
            for k in (0, 1):
                column = pl.multiple_of(half * 3584 + k * 1792 + t * 256, 256)
                both.append(jnp.dot(
                    head_out[...], out_w[:, pl.ds(column, 256)], preferred_element_type=jnp.float32
                ).reshape(16, 8, 256))
            tile = jnp.concatenate(both, axis=1).astype(jnp.bfloat16)
            if half == 0:
                part[0, :, :, pl.ds(lane, 256)] = tile
            else:
                for p in range(16):
                    part[1, (p % 4) * 4 + p // 4, :, pl.ds(lane, 256)] = tile[p]
            return 0

        lax.fori_loop(0, 7, project, 0)
        for d in (1, 2, 3):
            to, line = (at_y(d), lax.rem(y + d, 4)) if half == 0 else (at_z(d), lax.rem(z + d, 4))
            copy = pltpu.make_async_remote_copy(
                src_ref=part.at[half, pl.ds(line * 4, 4)], dst_ref=part_in.at[half, d - 1],
                send_sem=r_send.at[half, 0, d - 1], recv_sem=r_recv.at[half, 0, d - 1],
                device_id=to, device_id_type=MESH,
            )
            copy.start()
            first.append(copy)
    second = []
    for half in (0, 1):
        for d in (1, 2, 3):
            first[half * 3 + d - 1].wait_recv()
        own = y if half == 0 else z

        def add(k, _):
            value = part[half, own * 4 + k].astype(jnp.float32)
            for d in range(3):
                value = value + part_in[half, d, k].astype(jnp.float32)
            summed[half, k] = value.astype(jnp.bfloat16)
            return 0

        lax.fori_loop(0, 4, add, 0)
        for d in (1, 2, 3):
            to, line = (at_z(d), lax.rem(z + d, 4)) if half == 0 else (at_y(d), lax.rem(y + d, 4))
            copy = pltpu.make_async_remote_copy(
                src_ref=summed.at[half, line], dst_ref=summed_in.at[half, d - 1],
                send_sem=r_send.at[half, 1, d - 1], recv_sem=r_recv.at[half, 1, d - 1],
                device_id=to, device_id_type=MESH,
            )
            copy.start()
            second.append(copy)
    squares = jnp.zeros((8, 1), jnp.float32)
    for half in (0, 1):
        for d in (1, 2, 3):
            second[half * 3 + d - 1].wait_recv()
        value = summed[half, z if half == 0 else y].astype(jnp.float32)
        for d in range(3):
            value = value + summed_in[half, d].astype(jnp.float32)
        for k in (0, 1):
            q = 2 * half + k
            row = residual[:, q * 1792:(q + 1) * 1792].astype(jnp.float32) + value[k * 8:(k + 1) * 8]
            rows[q] = row
            mixed[:, q * 1792:(q + 1) * 1792] = row
            squares = squares + jnp.sum(row * row, axis=1, keepdims=True)
    norm = lax.rsqrt(squares / 7168.0 + 1e-06)
    for q in (0, 2):
        pair = jnp.concatenate([rows[q] * norm, rows[q + 1] * norm], axis=0)
        normed[q * 8:(q + 2) * 8] = pair.astype(jnp.bfloat16)

    for copy in sent + first + second:
        copy.wait_send()
    for half in (0, 1):
        for group in range(5):
            for kind in range(4):
                gather_copy(half, group if group < 4 else None, kind, e).wait_send()


def attend_call(served, queries, chosen, w_uv, w_out, residual, w_down):
    vmem = pl.BlockSpec(memory_space=pltpu.VMEM)
    anywhere = pl.BlockSpec(memory_space=pl.ANY)
    bf16, f32 = jnp.bfloat16, jnp.float32
    dma = pltpu.SemaphoreType.DMA
    return pl.pallas_call(
        attend_kernel,
        name="attend",
        out_shape=(
            jax.ShapeDtypeStruct((8, 7168), f32),
            jax.ShapeDtypeStruct((32, 1792), bf16),
            jax.ShapeDtypeStruct((2048, 896), bf16),
        ),
        in_specs=[vmem, vmem, vmem, vmem, anywhere, vmem, anywhere],
        out_specs=(vmem, vmem, anywhere),
        scratch_shapes=[
            pltpu.VMEM((16, 256, 576), bf16),
            pltpu.VMEM((4, 128, 576), bf16),
            pltpu.VMEM((4, 128, 256), f32),
            pltpu.VMEM((4, 128, 128), f32),
            pltpu.VMEM((4, 128, 128), f32),
            pltpu.VMEM((4, 128, 512), f32),
            pltpu.VMEM((128, 512), bf16),
            pltpu.VMEM((512, 7168), bf16),
            pltpu.VMEM((2, 16, 16, 1792), bf16),
            pltpu.VMEM((2, 3, 4, 16, 1792), bf16),
            pltpu.VMEM((2, 4, 16, 1792), bf16),
            pltpu.VMEM((2, 3, 16, 1792), bf16),
            pltpu.VMEM((4, 8, 1792), f32),
            dma((7,)), dma((7,)),
            dma((2, 5, 4)), dma((2, 5, 4)),
            dma((2, 2, 3)), dma((2, 2, 3)),
            dma((7,)), dma((7,)),
            dma((2,)),
        ],
        compiler_params=pltpu.CompilerParams(
            collective_id=0, has_side_effects=True, vmem_limit_bytes=56 << 20
        ),
    )(served, queries, chosen, w_uv, w_out, residual, w_down)


def serve(latent_store, group_passages, passage_place):
    s, e = lax.axis_index("store"), lax.axis_index("ep")
    lists = group_passages.reshape(8, 8, 4)
    ids = lax.dynamic_slice(lists, (0, s, e // 4), (8, 1, 1)).reshape(8)
    places = passage_place[ids] - s * 32
    return jax.vmap(
        lambda row: lax.dynamic_slice(latent_store, (row, (e % 4) * 32, 0), (1, 32, 576))[0]
    )(places)


def front(queries, residual_in, latent_store, group_passages, row_slots, passage_place, w_uv, w_out, w_down):
    served = serve(latent_store, group_passages, passage_place)
    chosen = jnp.any(row_slots[:, :, None] == jnp.arange(32, dtype=jnp.int32), axis=1).astype(jnp.bfloat16)
    return attend_call(served, queries, chosen, w_uv, w_out, residual_in, w_down[0])


def build_slots(chosen_ids, expert_count, capacity):
    expert_range = jnp.arange(expert_count, dtype=jnp.int32)
    routed = jnp.sum((chosen_ids[..., None] == expert_range).astype(jnp.int32), axis=-2)
    earlier = jnp.cumsum(routed, axis=-2) - routed
    depth_range = jnp.arange(capacity, dtype=jnp.int32)
    slot_mask = (routed[..., None] == 1) & (earlier[..., None] == depth_range)
    return jnp.moveaxis(slot_mask, -3, -1)


def body(
    queries, residual_in, latent_store, group_passages, row_slots, passage_place, w_uv, w_out,
    expert_ids, expert_gates, w_gate, w_up, w_down,
):
    mixed_rows, normed, _ = front(
        queries, residual_in, latent_store, group_passages, row_slots, passage_place, w_uv, w_out, w_down
    )
    normed = normed.reshape(4, 8, 1792).transpose(1, 0, 2).reshape(8, 7168)
    expert_count, tok_rows, model_width, top_count = 16, 8, 7168, 4
    capacity = min(tok_rows, 2 * ((tok_rows * top_count + expert_count - 1) // expert_count))
    slot_table = build_slots(expert_ids, expert_count, capacity).astype(jnp.bfloat16)
    outgoing = jnp.einsum(
        "ecr,rd->ecd", slot_table, normed, preferred_element_type=jnp.float32
    ).astype(jnp.bfloat16)
    arrived = lax.all_to_all(outgoing, "ep", split_axis=0, concat_axis=0, tiled=True)
    gathered = lax.all_gather(
        arrived.reshape(expert_count * capacity, model_width), "store", axis=0, tiled=True
    )
    row_block = gathered
    gate_proj = jnp.dot(row_block, w_gate[0], preferred_element_type=jnp.float32)
    up_proj = jnp.dot(row_block, w_up[0], preferred_element_type=jnp.float32)
    hidden = (jax.nn.silu(gate_proj) * up_proj).astype(jnp.bfloat16)
    summed = lax.psum_scatter(
        jnp.dot(hidden, w_down[0], preferred_element_type=jnp.float32).astype(jnp.bfloat16),
        "store",
        scatter_dimension=0,
        tiled=True,
    )
    expert_rows = summed.reshape(expert_count, capacity, model_width)
    returned = lax.all_to_all(expert_rows, "ep", split_axis=0, concat_axis=0, tiled=True)
    expert_range = jnp.arange(expert_count, dtype=jnp.int32)
    gate_of = jnp.sum(
        jnp.where(expert_ids[:, :, None] == expert_range, expert_gates[:, :, None], 0.0), axis=1
    )
    weighted = slot_table.astype(jnp.float32) * jnp.transpose(gate_of)[:, None, :]
    expert_mix = jnp.einsum(
        "ecr,ecd->rd", weighted, returned.astype(jnp.float32), precision=lax.Precision.HIGHEST
    )
    return (mixed_rows + expert_mix).astype(jnp.bfloat16)


def solution(mesh):
    return jax.shard_map(
        body,
        mesh=mesh,
        in_specs=(
            P("store", "ep"),
            P(("store", "ep"), None),
            P("store", None, None),
            P(),
            P("store", None),
            P(),
            P("ep", None, None),
            P("ep", None),
            P(("store", "ep"), None),
            P(("store", "ep"), None),
            P("ep", None, "store"),
            P("ep", None, "store"),
            P("ep", "store", None),
        ),
        out_specs=P(("store", "ep"), None),
        check_vma=False,
    )
```

```python
import functools

import jax
import jax.numpy as jnp
from jax import lax
from jax.experimental import pallas as pl
from jax.experimental.pallas import tpu as pltpu
from jax.sharding import PartitionSpec as P

score_scale = 192.0 ** (-0.5)
MESH = pl.DeviceIdType.MESH
LOW = -1e30


def offset_of(i):
    return i + i // 2 - 2 * (i // 3)


def attend_kernel(
    served, queries, chosen, w_uv, w_out, residual, w_down,
    mixed, normed, down_cols,
    kv, heads, mask, top, total, acc, head_out, out_w, part, part_in, summed, summed_in, rows,
    x_send, x_recv, g_send, g_recv, r_send, r_recv, d_send, d_recv, w_sem,
):
    s = lax.axis_index("store")
    e = lax.axis_index("ep")
    y, z = e // 4, e % 4

    def at_y(d):
        return (s, lax.rem(y + d, 4) * 4 + z)

    def at_z(d):
        return (s, y * 4 + lax.rem(z + d, 4))

    def at_s(d):
        return (lax.rem(s + d, 8), e)

    peers = [at_s(d) for d in range(1, 8)] + [at_y(d) for d in (1, 2, 3)] + [at_z(d) for d in (1, 2, 3)]
    barrier = pltpu.get_barrier_semaphore()
    for peer in peers:
        pl.semaphore_signal(barrier, inc=1, device_id=peer, device_id_type=MESH)
    get_w = pltpu.make_async_copy(w_out, out_w, w_sem.at[0])
    get_w.start()
    pl.semaphore_wait(barrier, len(peers))

    sent = []
    for d in range(1, 8):
        to = at_s(d)
        copy = pltpu.make_async_remote_copy(
            src_ref=served.at[to[0]],
            dst_ref=kv.at[e, pl.ds(pl.multiple_of(s * 32, 32), 32)],
            send_sem=x_send.at[d - 1], recv_sem=x_recv.at[d - 1],
            device_id=to, device_id_type=MESH,
        )
        copy.start()
        sent.append(copy)
    kv[e, pl.ds(pl.multiple_of(s * 32, 32), 32)] = served[s]

    for h in range(4):
        heads[h] = queries[:, h * 576:(h + 1) * 576]
    slot_row = lax.broadcasted_iota(jnp.int32, (32, 256), 0)
    token_col = lax.broadcasted_iota(jnp.int32, (32, 256), 1)
    for j in range(4):
        spread = (slot_row == (token_col // 32) * 4 + j).astype(jnp.bfloat16)
        mask[j] = jnp.dot(chosen[...], spread, preferred_element_type=jnp.float32)
    top[...] = jnp.full_like(top, LOW)
    total[...] = jnp.zeros_like(total)
    acc[...] = jnp.zeros_like(acc)

    def chunk(half, first, second):
        dy, dz = (first, second) if half == 0 else (second, first)
        return lax.rem(y - dy + 4, 4) * 4 + lax.rem(z - dz + 4, 4)

    def attend(p_a, p_b):
        keys = jnp.concatenate([kv[p_a, 0:128], kv[p_b, 128:256]], axis=0)
        live = jnp.concatenate([mask[p_a // 4][:, 0:128], mask[p_b // 4][:, 128:256]], axis=1)
        for h in range(4):
            scores = lax.dot_general(
                heads[h], keys, (((1,), (1,)), ((), ())), preferred_element_type=jnp.float32
            ) * score_scale
            scores = jnp.where(live > 0.5, scores, LOW)
            old = top[h]
            new = jnp.maximum(old, jnp.max(scores, axis=1, keepdims=True))
            exponent = jnp.exp(scores - new[:, 0:1]) * live
            scale = jnp.exp(old - new)
            top[h] = new
            total[h] = total[h] * scale + jnp.sum(exponent, axis=1, keepdims=True)
            acc[h] = acc[h] * scale[:, 0:1] + jnp.dot(
                exponent.astype(jnp.bfloat16), keys[:, 0:512], preferred_element_type=jnp.float32
            )

    def gather_copy(half, group, kind, place):
        low = half * 128 + (64 if kind == 3 else 0)
        size = 64 if kind >= 2 else 128
        on_y = (half == 0) == (group is None)
        to = (at_y if on_y else at_z)(1 if kind % 2 == 0 else 3)
        block = kv.at[place, pl.ds(low, size)]
        index = 4 if group is None else group
        return pltpu.make_async_remote_copy(
            src_ref=block, dst_ref=block,
            send_sem=g_send.at[half, index, kind], recv_sem=g_recv.at[half, index, kind],
            device_id=to, device_id_type=MESH,
        )

    def launch(group, offset):
        for half in (0, 1):
            for kind in (0, 1):
                gather_copy(half, group, kind, chunk(half, offset, 0)).start()

    for copy in sent:
        copy.wait_recv()
    launch(None, 0)
    launch(0, 0)
    keep_w = pltpu.make_async_copy(
        w_down.at[:, pl.ds(pl.multiple_of(s * 896, 896), 896)],
        down_cols.at[pl.ds(pl.multiple_of(s * 256, 256), 256)], w_sem.at[1],
    )
    keep_w.start()
    moved = []
    for d in range(1, 8):
        to = at_s(d)
        copy = pltpu.make_async_remote_copy(
            src_ref=w_down.at[:, pl.ds(pl.multiple_of(to[0] * 896, 896), 896)],
            dst_ref=down_cols.at[pl.ds(pl.multiple_of(s * 256, 256), 256)],
            send_sem=d_send.at[d - 1], recv_sem=d_recv.at[d - 1],
            device_id=to, device_id_type=MESH,
        )
        copy.start()
        moved.append(copy)
    attend(e, e)
    for kind in (0, 1):
        offset = 1 if kind == 0 else 3
        for half in (0, 1):
            gather_copy(half, None, kind, e).wait_recv()
            gather_copy(half, None, kind + 2, chunk(half, offset, 0)).start()
        launch(kind + 1, offset)

    def near(i, _):
        offset = 1 + 2 * i
        attend(chunk(0, offset, 0), chunk(1, offset, 0))
        return 0

    lax.fori_loop(0, 2, near, 0)
    for half in (0, 1):
        for kind in (2, 3):
            gather_copy(half, None, kind, e).wait_recv()
    launch(3, 2)
    attend(chunk(0, 2, 0), chunk(1, 2, 0))

    def sides(i, _):
        offset = offset_of(i)
        for kind in (0, 1):
            back = 1 if kind == 0 else 3
            for half in (0, 1):
                gather_copy(half, i, kind, e).wait_recv()
                gather_copy(half, i, kind + 2, chunk(half, offset, back)).start()

        def both(k, _):
            attend(chunk(0, offset, 1 + 2 * k), chunk(1, offset, 1 + 2 * k))
            return 0

        lax.fori_loop(0, 2, both, 0)
        return 0

    lax.fori_loop(0, 4, sides, 0)

    def far(i, _):
        offset = offset_of(i)
        for half in (0, 1):
            for kind in (2, 3):
                gather_copy(half, i, kind, e).wait_recv()
        attend(chunk(0, offset, 2), chunk(1, offset, 2))
        return 0

    lax.fori_loop(0, 4, far, 0)

    for h in range(4):
        latent = (acc[h] / total[h][:, 0:1]).astype(jnp.bfloat16)
        head_out[:, h * 128:(h + 1) * 128] = jnp.dot(
            latent, w_uv[h], preferred_element_type=jnp.float32
        ).astype(jnp.bfloat16)
    get_w.wait()

    first = []
    for half in (0, 1):
        def project(t, _):
            lane = pl.multiple_of(t * 256, 256)
            both = []
            for k in (0, 1):
                column = pl.multiple_of(half * 3584 + k * 1792 + t * 256, 256)
                both.append(jnp.dot(
                    head_out[...], out_w[:, pl.ds(column, 256)], preferred_element_type=jnp.float32
                ).reshape(16, 8, 256))
            tile = jnp.concatenate(both, axis=1).astype(jnp.bfloat16)
            if half == 0:
                part[0, :, :, pl.ds(lane, 256)] = tile
            else:
                for p in range(16):
                    part[1, (p % 4) * 4 + p // 4, :, pl.ds(lane, 256)] = tile[p]
            return 0

        lax.fori_loop(0, 7, project, 0)
        for d in (1, 2, 3):
            to, line = (at_y(d), lax.rem(y + d, 4)) if half == 0 else (at_z(d), lax.rem(z + d, 4))
            copy = pltpu.make_async_remote_copy(
                src_ref=part.at[half, pl.ds(line * 4, 4)], dst_ref=part_in.at[half, d - 1],
                send_sem=r_send.at[half, 0, d - 1], recv_sem=r_recv.at[half, 0, d - 1],
                device_id=to, device_id_type=MESH,
            )
            copy.start()
            first.append(copy)
    second = []
    for half in (0, 1):
        for d in (1, 2, 3):
            first[half * 3 + d - 1].wait_recv()
        own = y if half == 0 else z

        def add(k, _):
            value = part[half, own * 4 + k].astype(jnp.float32)
            for d in range(3):
                value = value + part_in[half, d, k].astype(jnp.float32)
            summed[half, k] = value.astype(jnp.bfloat16)
            return 0

        lax.fori_loop(0, 4, add, 0)
        for d in (1, 2, 3):
            to, line = (at_z(d), lax.rem(z + d, 4)) if half == 0 else (at_y(d), lax.rem(y + d, 4))
            copy = pltpu.make_async_remote_copy(
                src_ref=summed.at[half, line], dst_ref=summed_in.at[half, d - 1],
                send_sem=r_send.at[half, 1, d - 1], recv_sem=r_recv.at[half, 1, d - 1],
                device_id=to, device_id_type=MESH,
            )
            copy.start()
            second.append(copy)
    squares = jnp.zeros((8, 1), jnp.float32)
    for half in (0, 1):
        for d in (1, 2, 3):
            second[half * 3 + d - 1].wait_recv()
        value = summed[half, z if half == 0 else y].astype(jnp.float32)
        for d in range(3):
            value = value + summed_in[half, d].astype(jnp.float32)
        for k in (0, 1):
            q = 2 * half + k
            row = residual[:, q * 1792:(q + 1) * 1792].astype(jnp.float32) + value[k * 8:(k + 1) * 8]
            rows[q] = row
            mixed[:, q * 1792:(q + 1) * 1792] = row
            squares = squares + jnp.sum(row * row, axis=1, keepdims=True)
    norm = lax.rsqrt(squares / 7168.0 + 1e-06)
    for q in (0, 2):
        pair = jnp.concatenate([rows[q] * norm, rows[q + 1] * norm], axis=0)
        normed[q * 8:(q + 2) * 8] = pair.astype(jnp.bfloat16)

    keep_w.wait()
    for copy in moved:
        copy.wait_recv()
    for copy in sent + first + second + moved:
        copy.wait_send()
    for half in (0, 1):
        for group in range(5):
            for kind in range(4):
                gather_copy(half, group if group < 4 else None, kind, e).wait_send()


def attend_call(served, queries, chosen, w_uv, w_out, residual, w_down):
    vmem = pl.BlockSpec(memory_space=pltpu.VMEM)
    anywhere = pl.BlockSpec(memory_space=pl.ANY)
    bf16, f32 = jnp.bfloat16, jnp.float32
    dma = pltpu.SemaphoreType.DMA
    return pl.pallas_call(
        attend_kernel,
        name="attend",
        out_shape=(
            jax.ShapeDtypeStruct((8, 7168), f32),
            jax.ShapeDtypeStruct((32, 1792), bf16),
            jax.ShapeDtypeStruct((2048, 896), bf16),
        ),
        in_specs=[vmem, vmem, vmem, vmem, anywhere, vmem, anywhere],
        out_specs=(vmem, vmem, anywhere),
        scratch_shapes=[
            pltpu.VMEM((16, 256, 576), bf16),
            pltpu.VMEM((4, 128, 576), bf16),
            pltpu.VMEM((4, 128, 256), f32),
            pltpu.VMEM((4, 128, 128), f32),
            pltpu.VMEM((4, 128, 128), f32),
            pltpu.VMEM((4, 128, 512), f32),
            pltpu.VMEM((128, 512), bf16),
            pltpu.VMEM((512, 7168), bf16),
            pltpu.VMEM((2, 16, 16, 1792), bf16),
            pltpu.VMEM((2, 3, 4, 16, 1792), bf16),
            pltpu.VMEM((2, 4, 16, 1792), bf16),
            pltpu.VMEM((2, 3, 16, 1792), bf16),
            pltpu.VMEM((4, 8, 1792), f32),
            dma((7,)), dma((7,)),
            dma((2, 5, 4)), dma((2, 5, 4)),
            dma((2, 2, 3)), dma((2, 2, 3)),
            dma((7,)), dma((7,)),
            dma((2,)),
        ],
        compiler_params=pltpu.CompilerParams(
            collective_id=0, has_side_effects=True, vmem_limit_bytes=56 << 20
        ),
    )(served, queries, chosen, w_uv, w_out, residual, w_down)


def serve(latent_store, group_passages, passage_place):
    s, e = lax.axis_index("store"), lax.axis_index("ep")
    lists = group_passages.reshape(8, 8, 4)
    ids = lax.dynamic_slice(lists, (0, s, e // 4), (8, 1, 1)).reshape(8)
    places = passage_place[ids] - s * 32
    return jax.vmap(
        lambda row: lax.dynamic_slice(latent_store, (row, (e % 4) * 32, 0), (1, 32, 576))[0]
    )(places)


def front(queries, residual_in, latent_store, group_passages, row_slots, passage_place, w_uv, w_out, w_down):
    served = serve(latent_store, group_passages, passage_place)
    chosen = jnp.any(row_slots[:, :, None] == jnp.arange(32, dtype=jnp.int32), axis=1).astype(jnp.bfloat16)
    return attend_call(served, queries, chosen, w_uv, w_out, residual_in, w_down[0])


def expert_kernel(
    normed, mixed, place, weigh, w_gate, w_up, down_cols,
    out,
    outgoing, arrived, x_rows, w_in, w_down, pre, hid, y_part, y_rows, back, returned,
    t_send, t_recv, a_send, a_recv, h_send, h_recv, y_send, y_recv, b_send, b_recv, w_sem,
):
    s = lax.axis_index("store")
    e = lax.axis_index("ep")
    y, z = e // 4, e % 4
    sibling = s + 1 - 2 * (s % 2)

    def on_store(d):
        return lax.rem(s + d, 8)

    def on_ep(dy, dz):
        return lax.rem(y + dy, 4) * 4 + lax.rem(z + dz, 4)

    barrier = pltpu.get_barrier_semaphore()
    peers = [(on_store(d), e) for d in range(1, 8)]
    peers += [(s, on_ep(dy, dz)) for dy in range(4) for dz in range(4) if dy or dz]
    for peer in peers:
        pl.semaphore_signal(barrier, inc=1, device_id=peer, device_id_type=MESH)
    loads = [
        pltpu.make_async_copy(w_gate, w_in.at[:, 0:256], w_sem.at[0]),
        pltpu.make_async_copy(w_up, w_in.at[:, 256:512], w_sem.at[1]),
        pltpu.make_async_copy(down_cols, w_down, w_sem.at[2]),
    ]
    for load in loads:
        load.start()
    outgoing[...] = jnp.dot(
        place[...], normed[...], preferred_element_type=jnp.float32
    ).astype(jnp.bfloat16).reshape(16, 16, 1792)
    pl.semaphore_wait(barrier, len(peers))

    def copy_to(src, dst, send, recv, device):
        return pltpu.make_async_remote_copy(
            src_ref=src, dst_ref=dst, send_sem=send, recv_sem=recv, device_id=device, device_id_type=MESH
        )

    def dispatch(k, dz):
        to = on_ep(offset_of(k), dz)
        return copy_to(outgoing.at[to], arrived.at[e], t_send.at[k, dz], t_recv.at[k, dz], (s, to))

    def give_back(k, dz):
        to = on_ep(4 - offset_of(k), dz)
        return copy_to(back.at[k, lax.rem(z + dz, 4)], returned.at[e], b_send.at[k, dz], b_recv.at[k, dz], (s, to))

    def gather(k, kind):
        to = {0: 2, 1: 6, 2: 2, 3: 6}.get(kind)
        to = sibling if to is None else on_store(to)
        block = on_store((0, 0, 6, 2, 0, 6, 2, 4, 4)[kind])
        low = pl.multiple_of(block * 16, 16)
        columns = {2: (0, 3584), 3: (3584, 3584), 7: (0, 3584), 8: (3584, 3584)}.get(kind, (0, 7168))
        ref = x_rows.at[k, pl.ds(low, 16), pl.ds(*columns)]
        return copy_to(ref, ref, a_send.at[k, kind], a_recv.at[k, kind], (to, e))

    def share(k, kind):
        to = on_store((2, 6, 4)[kind]) if kind < 3 else sibling
        block = on_store((0, 0, 0, 0, 6, 2, 4)[kind])
        ref = hid.at[k, :, pl.ds(pl.multiple_of(block * 256, 256), 256)]
        return copy_to(ref, ref, h_send.at[k, kind], h_recv.at[k, kind], (to, e))

    def hand_over(k, d):
        to = on_store(d)
        return copy_to(
            y_part.at[k, pl.ds(pl.multiple_of(to * 16, 16), 16)],
            y_rows.at[k, :, pl.ds(pl.multiple_of(s * 896, 896), 896)],
            y_send.at[k, d - 1], y_recv.at[k, d - 1], (to, e),
        )

    for k in range(4):
        for dz in (0, 1, 3, 2):
            if k or dz:
                dispatch(k, dz).start()
    arrived[e] = outgoing[e]

    rows16 = lax.broadcasted_iota(jnp.int32, (16, 64), 0)
    cols64 = lax.broadcasted_iota(jnp.int32, (16, 64), 1)
    rows64 = lax.broadcasted_iota(jnp.int32, (64, 16), 0)
    cols16 = lax.broadcasted_iota(jnp.int32, (64, 16), 1)

    def take(q):
        return (cols64 == (rows16 // 4) * 16 + q * 4 + rows16 % 4).astype(jnp.bfloat16)

    def put(q):
        return (rows64 == (cols16 // 4) * 16 + q * 4 + cols16 % 4).astype(jnp.bfloat16)

    def enter(k):
        for dz in range(1, 4):
            dispatch(k, dz).wait_recv()

        @pl.when(k > 0)
        def _():
            dispatch(k, 0).wait_recv()

        line = lax.rem(y + 4 - offset_of(k), 4)
        block = arrived[pl.ds(line * 4, 4)].reshape(64, 1792)
        for q in range(4):
            x_rows[k, pl.ds(pl.multiple_of(s * 16, 16), 16), q * 1792:(q + 1) * 1792] = jnp.dot(
                take(q), block, preferred_element_type=jnp.float32
            ).astype(jnp.bfloat16)
        for kind in (0, 1, 4):
            gather(k, kind).start()

    def pass_on(k):
        for kind in (0, 1):
            gather(k, kind).wait_recv()
            gather(k, kind + 2).start()
            gather(k, kind + 5).start()

    def hidden(k):
        for kind in (2, 3):
            gather(k, kind).wait_recv()
            gather(k, kind + 5).start()
        for kind in range(4, 9):
            gather(k, kind).wait_recv()
        pre[...] = jnp.zeros_like(pre)

        def add(q, _):
            low = pl.multiple_of(q * 1792, 1792)
            pre[...] += jnp.dot(
                x_rows[k, :, pl.ds(low, 1792)], w_in[pl.ds(low, 1792)], preferred_element_type=jnp.float32
            )
            return 0

        lax.fori_loop(0, 4, add, 0)
        gate = pre[:, 0:256]
        hid[k, :, pl.ds(pl.multiple_of(s * 256, 256), 256)] = (
            gate / (1.0 + jnp.exp(-gate)) * pre[:, 256:512]
        ).astype(jnp.bfloat16)
        for kind in range(4):
            share(k, kind).start()

    def project(k):
        for kind in range(3):
            share(k, kind).wait_recv()
            share(k, kind + 4).start()
        for kind in range(3, 7):
            share(k, kind).wait_recv()
        y_part[k] = jnp.dot(hid[k], w_down[...], preferred_element_type=jnp.float32).astype(jnp.bfloat16)
        for d in range(1, 8):
            hand_over(k, d).start()
        y_rows[k, :, pl.ds(pl.multiple_of(s * 896, 896), 896)] = y_part[k, pl.ds(pl.multiple_of(s * 16, 16), 16)]

    def leave(k):
        for d in range(1, 8):
            hand_over(k, d).wait_recv()
        total = jnp.zeros((64, 1792), jnp.float32)
        for q in range(4):
            total = total + jnp.dot(
                put(q), y_rows[k, :, q * 1792:(q + 1) * 1792], preferred_element_type=jnp.float32
            )
        back[k] = total.astype(jnp.bfloat16).reshape(4, 16, 1792)
        for dz in range(1, 4):
            give_back(k, dz).start()

        @pl.when(k > 0)
        def _():
            give_back(k, 0).start()

        @pl.when(k == 0)
        def _():
            returned[e] = back[k, z]

    def step(t, _):
        @pl.when(t < 4)
        def _():
            enter(t)

        @pl.when(t == 1)
        def _():
            for load in loads:
                load.wait()

        @pl.when((t >= 1) & (t < 5))
        def _():
            hidden(t - 1)

        @pl.when(t < 4)
        def _():
            pass_on(t)

        @pl.when((t >= 2) & (t < 6))
        def _():
            project(t - 2)

        @pl.when(t >= 3)
        def _():
            leave(t - 3)

        return 0

    lax.fori_loop(0, 7, step, 0)

    for k in range(4):
        for dz in range(4):
            if k or dz:
                give_back(k, dz).wait_recv()
    rows = returned[...].reshape(256, 1792)
    total = jnp.dot(weigh[0], rows, preferred_element_type=jnp.float32) + jnp.dot(
        weigh[1], rows, preferred_element_type=jnp.float32
    )
    for q in range(4):
        out[:, q * 1792:(q + 1) * 1792] = (
            mixed[:, q * 1792:(q + 1) * 1792] + total[q * 8:(q + 1) * 8]
        ).astype(jnp.bfloat16)

    for k in range(4):
        for dz in range(4):
            if k or dz:
                dispatch(k, dz).wait_send()
                give_back(k, dz).wait_send()
        for kind in range(9):
            gather(k, kind).wait_send()
        for kind in range(7):
            share(k, kind).wait_send()
            hand_over(k, kind + 1).wait_send()


def expert_call(normed, mixed, place, weigh, w_gate, w_up, down_cols):
    vmem = pl.BlockSpec(memory_space=pltpu.VMEM)
    anywhere = pl.BlockSpec(memory_space=pl.ANY)
    bf16, f32 = jnp.bfloat16, jnp.float32
    dma = pltpu.SemaphoreType.DMA
    return pl.pallas_call(
        expert_kernel,
        name="experts",
        out_shape=jax.ShapeDtypeStruct((8, 7168), bf16),
        in_specs=[vmem, vmem, vmem, vmem, anywhere, anywhere, anywhere],
        out_specs=vmem,
        scratch_shapes=[
            pltpu.VMEM((16, 16, 1792), bf16),
            pltpu.VMEM((16, 16, 1792), bf16),
            pltpu.VMEM((4, 128, 7168), bf16),
            pltpu.VMEM((7168, 512), bf16),
            pltpu.VMEM((2048, 896), bf16),
            pltpu.VMEM((128, 512), f32),
            pltpu.VMEM((4, 128, 2048), bf16),
            pltpu.VMEM((4, 128, 896), bf16),
            pltpu.VMEM((4, 16, 7168), bf16),
            pltpu.VMEM((4, 4, 16, 1792), bf16),
            pltpu.VMEM((16, 16, 1792), bf16),
            dma((4, 4)), dma((4, 4)),
            dma((4, 9)), dma((4, 9)),
            dma((4, 7)), dma((4, 7)),
            dma((4, 7)), dma((4, 7)),
            dma((4, 4)), dma((4, 4)),
            dma((3,)),
        ],
        compiler_params=pltpu.CompilerParams(
            collective_id=1, has_side_effects=True, vmem_limit_bytes=56 << 20
        ),
    )(normed, mixed, place, weigh, w_gate, w_up, down_cols)


def routing(expert_ids, expert_gates):
    experts = jnp.arange(16, dtype=jnp.int32)
    named = (expert_ids[:, :, None] == experts).astype(jnp.float32)
    routed = jnp.sum(named, axis=1)
    gate = jnp.sum(named * expert_gates[:, :, None], axis=1)
    earlier = jnp.cumsum(routed, axis=0) - routed
    depth = jnp.arange(4, dtype=jnp.float32)
    slot = jnp.where((routed[..., None] > 0.5) & (earlier[..., None] == depth), 1.0, 0.0)
    eye = jnp.eye(4, dtype=jnp.float32)
    place = jnp.einsum("rec,qp->eqcpr", slot, eye).reshape(256, 32).astype(jnp.bfloat16)
    held = slot * gate[..., None]
    high = held.astype(jnp.bfloat16)
    low = (held - high.astype(jnp.float32)).astype(jnp.bfloat16)
    weigh = jnp.stack([high, low]).astype(jnp.float32)
    weigh = jnp.einsum("nrec,qp->nqrepc", weigh, eye).reshape(2, 32, 256).astype(jnp.bfloat16)
    return place, weigh


def body(
    queries, residual_in, latent_store, group_passages, row_slots, passage_place, w_uv, w_out,
    expert_ids, expert_gates, w_gate, w_up, w_down,
):
    mixed, normed, down_cols = front(
        queries, residual_in, latent_store, group_passages, row_slots, passage_place, w_uv, w_out, w_down
    )
    place, weigh = routing(expert_ids, expert_gates)
    return expert_call(normed, mixed, place, weigh, w_gate[0], w_up[0], down_cols)


def solution(mesh):
    return jax.shard_map(
        body,
        mesh=mesh,
        in_specs=(
            P("store", "ep"),
            P(("store", "ep"), None),
            P("store", None, None),
            P(),
            P("store", None),
            P(),
            P("ep", None, None),
            P("ep", None),
            P(("store", "ep"), None),
            P(("store", "ep"), None),
            P("ep", None, "store"),
            P("ep", None, "store"),
            P("ep", "store", None),
        ),
        out_specs=P(("store", "ep"), None),
        check_vma=False,
    )
```

```python
import functools

import jax
import jax.numpy as jnp
from jax import lax
from jax.experimental import pallas as pl
from jax.experimental.pallas import tpu as pltpu
from jax.sharding import PartitionSpec as P

SCALE = 192.0 ** (-0.5) * 1.4426950408889634
MESH = pl.DeviceIdType.MESH
LOW = -1e29
FAR_LOW = 1e30


def offset_of(i):
    return i + i // 2 - 2 * (i // 3)


def attend_kernel(
    served, served_far, queries, row_slots, w_uv, w_out, residual, w_down,
    mixed, normed, down_cols,
    kv, heads, mask, top, total, acc, head_out, out_w, part, part_in, summed, summed_in, rows,
    x_send, x_recv, g_send, g_recv, r_send, r_recv, d_send, d_recv, w_sem,
):
    s = lax.axis_index("store")
    e = lax.axis_index("ep")
    y, z = e // 4, e % 4

    def at_y(d):
        return (s, lax.rem(y + d, 4) * 4 + z)

    def at_z(d):
        return (s, y * 4 + lax.rem(z + d, 4))

    def at_s(d):
        return (lax.rem(s + d, 8), e)

    def quarter(q):
        return pl.ds(pl.multiple_of(q * 144, 16), 144)

    peers = [at_s(d) for d in range(1, 8)] + [at_y(d) for d in (1, 2, 3)] + [at_z(d) for d in (1, 2, 3)]
    barrier = pltpu.get_barrier_semaphore()
    for peer in peers:
        pl.semaphore_signal(barrier, inc=1, device_id=peer, device_id_type=MESH)
    get_w = pltpu.make_async_copy(w_out, out_w, w_sem.at[0])
    get_w.start()
    pl.semaphore_wait(barrier, len(peers))

    sent = []
    for d in range(1, 8):
        to = at_s(d)
        copy = pltpu.make_async_remote_copy(
            src_ref=served.at[to[0]], dst_ref=kv.at[y, s, quarter(z)],
            send_sem=x_send.at[0, d - 1], recv_sem=x_recv.at[0, d - 1],
            device_id=to, device_id_type=MESH,
        )
        copy.start()
        sent.append(copy)
    keep = pltpu.make_async_copy(served.at[s], kv.at[y, s, quarter(z)], w_sem.at[2])
    keep.start()

    def far_copies(whole):
        def target(ref):
            return ref.at[lax.rem(y + 2, 4), s] if whole else ref.at[:, s, quarter(lax.rem(z + 2, 4))]

        def source(g):
            return served_far.at[g].reshape(576, 128) if whole else served_far.at[g]

        return [
            pltpu.make_async_remote_copy(
                src_ref=source(at_s(d)[0]), dst_ref=target(kv),
                send_sem=x_send.at[1, d - 1], recv_sem=x_recv.at[1, d - 1],
                device_id=at_s(d), device_id_type=MESH,
            )
            for d in range(1, 8)
        ] + [pltpu.make_async_copy(source(s), target(kv), w_sem.at[3])]

    def each_far(act):
        for whole in (False, True):
            @pl.when((s >= 4) if whole else (s < 4))
            def _():
                for copy in far_copies(whole):
                    act(copy)

    for h in range(4):
        heads[h * 128:(h + 1) * 128] = queries[:, h * 576:(h + 1) * 576]
    slot = lax.broadcasted_iota(jnp.int32, (32, 128), 0)
    chosen = jnp.zeros((32, 128), jnp.bool_)
    for i in range(16):
        chosen = chosen | (row_slots[i:i + 1] == slot)
    chosen = chosen.astype(jnp.bfloat16)
    slot_row = lax.broadcasted_iota(jnp.int32, (32, 512), 0)
    token_col = lax.broadcasted_iota(jnp.int32, (32, 512), 1)
    for j in range(4):
        for half in (0, 1):
            spread = (slot_row == (token_col // 128 + 4 * half) * 4 + j).astype(jnp.bfloat16)
            live = lax.dot_general(
                chosen, spread, (((0,), (0,)), ((), ())), preferred_element_type=jnp.float32
            )
            mask[j, half] = (live - 1.0) * FAR_LOW
    top[...] = jnp.full_like(top, LOW)
    total[...] = jnp.zeros_like(total)
    acc[...] = jnp.zeros_like(acc)

    def chunk(half, first, second):
        dy, dz = (first, second) if half == 0 else (second, first)
        return lax.rem(y - dy + 4, 4), lax.rem(z - dz + 4, 4)

    def attend(j, half):
        keys = jnp.concatenate([kv[j, half * 4 + i] for i in range(4)], axis=1)
        scores = jnp.dot(heads[...], keys, preferred_element_type=jnp.float32) * SCALE
        scores = (scores.reshape(4, 128, 512) + mask[j, half]).reshape(512, 512)
        old = top[...]
        new = jnp.maximum(old, jnp.max(scores, axis=1, keepdims=True))
        exponent = jnp.exp2(scores - new[:, 0:1])
        scale = jnp.exp2(old - new)
        top[...] = new
        total[...] = total[...] * scale + jnp.sum(exponent, axis=1, keepdims=True)
        acc[...] = acc[...] * scale[:, 0:1] + lax.dot_general(
            exponent.astype(jnp.bfloat16), keys[0:512], (((1,), (1,)), ((), ())),
            preferred_element_type=jnp.float32,
        )

    def gather_copy(half, group, kind, place):
        low = half * 4 + (2 if kind == 3 else 0)
        size = 2 if kind >= 2 else 4
        on_y = (half == 0) == (group is None)
        to = (at_y if on_y else at_z)(1 if kind % 2 == 0 else 3)
        block = kv.at[place[0], pl.ds(low, size), quarter(place[1])]
        index = 4 if group is None else group
        return pltpu.make_async_remote_copy(
            src_ref=block, dst_ref=block,
            send_sem=g_send.at[half, index, kind], recv_sem=g_recv.at[half, index, kind],
            device_id=to, device_id_type=MESH,
        )

    def launch(group, offset):
        for half in (0, 1):
            for kind in (0, 1):
                gather_copy(half, group, kind, chunk(half, offset, 0)).start()

    keep.wait()
    for copy in sent:
        copy.wait_recv()
    launch(None, 0)
    launch(0, 0)
    each_far(lambda copy: copy.start())
    keep_w = pltpu.make_async_copy(
        w_down.at[:, pl.ds(pl.multiple_of(s * 896, 896), 896)],
        down_cols.at[pl.ds(pl.multiple_of(s * 256, 256), 256)], w_sem.at[1],
    )
    keep_w.start()
    moved = []
    for d in range(1, 8):
        to = at_s(d)
        copy = pltpu.make_async_remote_copy(
            src_ref=w_down.at[:, pl.ds(pl.multiple_of(to[0] * 896, 896), 896)],
            dst_ref=down_cols.at[pl.ds(pl.multiple_of(s * 256, 256), 256)],
            send_sem=d_send.at[d - 1], recv_sem=d_recv.at[d - 1],
            device_id=to, device_id_type=MESH,
        )
        copy.start()
        moved.append(copy)
    for kind in (0, 1):
        offset = 1 if kind == 0 else 3
        for half in (0, 1):
            gather_copy(half, None, kind, (y, z)).wait_recv()
            gather_copy(half, None, kind + 2, chunk(half, offset, 0)).start()
        launch(kind + 1, offset)
    for half in (0, 1):
        for kind in (2, 3):
            gather_copy(half, None, kind, (y, z)).wait_recv()
    launch(3, 2)
    attend(y, 1)

    def take_far(copy):
        if copy.is_remote:
            copy.wait_recv()
        else:
            copy.wait()

    each_far(take_far)
    attend(lax.rem(y + 2, 4), 1)

    def sides(i, _):
        for kind in (0, 1):
            for half in (0, 1):
                gather_copy(half, i, kind, (y, z)).wait_recv()
        attend(chunk(0, offset_of(i), 0)[0], 0)
        return 0

    lax.fori_loop(0, 4, sides, 0)

    def last(i, _):
        attend(lax.rem(y + 1 + 2 * i, 4), 1)
        return 0

    lax.fori_loop(0, 2, last, 0)

    for h in range(4):
        own = pl.ds(h * 128, 128)
        latent = (acc[own] / total[own, 0:1]).astype(jnp.bfloat16)
        head_out[:, h * 128:(h + 1) * 128] = jnp.dot(
            latent, w_uv[h], preferred_element_type=jnp.float32
        ).astype(jnp.bfloat16)
    get_w.wait()

    first = []
    for half in (0, 1):
        def project(t, _):
            lane = pl.multiple_of(t * 256, 256)
            both = []
            for k in (0, 1):
                column = pl.multiple_of(half * 3584 + k * 1792 + t * 256, 256)
                both.append(jnp.dot(
                    head_out[...], out_w[:, pl.ds(column, 256)], preferred_element_type=jnp.float32
                ).reshape(16, 8, 256))
            tile = jnp.concatenate(both, axis=1).astype(jnp.bfloat16)
            if half == 0:
                part[0, :, :, pl.ds(lane, 256)] = tile
            else:
                for p in range(16):
                    part[1, (p % 4) * 4 + p // 4, :, pl.ds(lane, 256)] = tile[p]
            return 0

        lax.fori_loop(0, 7, project, 0)
        for d in (1, 2, 3):
            to, line = (at_y(d), lax.rem(y + d, 4)) if half == 0 else (at_z(d), lax.rem(z + d, 4))
            copy = pltpu.make_async_remote_copy(
                src_ref=part.at[half, pl.ds(line * 4, 4)], dst_ref=part_in.at[half, d - 1],
                send_sem=r_send.at[half, 0, d - 1], recv_sem=r_recv.at[half, 0, d - 1],
                device_id=to, device_id_type=MESH,
            )
            copy.start()
            first.append(copy)
    second = []
    for half in (0, 1):
        for d in (1, 2, 3):
            first[half * 3 + d - 1].wait_recv()
        own = y if half == 0 else z

        def add(k, _):
            value = part[half, own * 4 + k].astype(jnp.float32)
            for d in range(3):
                value = value + part_in[half, d, k].astype(jnp.float32)
            summed[half, k] = value.astype(jnp.bfloat16)
            return 0

        lax.fori_loop(0, 4, add, 0)
        for d in (1, 2, 3):
            to, line = (at_z(d), lax.rem(z + d, 4)) if half == 0 else (at_y(d), lax.rem(y + d, 4))
            copy = pltpu.make_async_remote_copy(
                src_ref=summed.at[half, line], dst_ref=summed_in.at[half, d - 1],
                send_sem=r_send.at[half, 1, d - 1], recv_sem=r_recv.at[half, 1, d - 1],
                device_id=to, device_id_type=MESH,
            )
            copy.start()
            second.append(copy)
    squares = jnp.zeros((8, 1), jnp.float32)
    for half in (0, 1):
        for d in (1, 2, 3):
            second[half * 3 + d - 1].wait_recv()
        value = summed[half, z if half == 0 else y].astype(jnp.float32)
        for d in range(3):
            value = value + summed_in[half, d].astype(jnp.float32)
        for k in (0, 1):
            q = 2 * half + k
            row = residual[:, q * 1792:(q + 1) * 1792].astype(jnp.float32) + value[k * 8:(k + 1) * 8]
            rows[q] = row
            mixed[:, q * 1792:(q + 1) * 1792] = row
            squares = squares + jnp.sum(row * row, axis=1, keepdims=True)
    norm = lax.rsqrt(squares / 7168.0 + 1e-06)
    for q in (0, 2):
        pair = jnp.concatenate([rows[q] * norm, rows[q + 1] * norm], axis=0)
        normed[q * 8:(q + 2) * 8] = pair.astype(jnp.bfloat16)

    keep_w.wait()
    for copy in moved:
        copy.wait_recv()
    for copy in sent + first + second + moved:
        copy.wait_send()
    each_far(lambda copy: copy.wait_send() if copy.is_remote else None)
    for half in (0, 1):
        for group in range(5):
            for kind in range(4 if group == 4 else 2):
                gather_copy(half, group if group < 4 else None, kind, (y, z)).wait_send()


def attend_call(served, served_far, queries, row_slots, w_uv, w_out, residual, w_down):
    vmem = pl.BlockSpec(memory_space=pltpu.VMEM)
    anywhere = pl.BlockSpec(memory_space=pl.ANY)
    bf16, f32 = jnp.bfloat16, jnp.float32
    dma = pltpu.SemaphoreType.DMA
    return pl.pallas_call(
        attend_kernel,
        name="attend",
        out_shape=(
            jax.ShapeDtypeStruct((8, 7168), f32),
            jax.ShapeDtypeStruct((32, 1792), bf16),
            jax.ShapeDtypeStruct((2048, 896), bf16),
        ),
        in_specs=[anywhere, anywhere, vmem, vmem, vmem, anywhere, vmem, anywhere],
        out_specs=(vmem, vmem, anywhere),
        scratch_shapes=[
            pltpu.VMEM((4, 8, 576, 128), bf16),
            pltpu.VMEM((512, 576), bf16),
            pltpu.VMEM((4, 2, 128, 512), f32),
            pltpu.VMEM((512, 128), f32),
            pltpu.VMEM((512, 128), f32),
            pltpu.VMEM((512, 512), f32),
            pltpu.VMEM((128, 512), bf16),
            pltpu.VMEM((512, 7168), bf16),
            pltpu.VMEM((2, 16, 16, 1792), bf16),
            pltpu.VMEM((2, 3, 4, 16, 1792), bf16),
            pltpu.VMEM((2, 4, 16, 1792), bf16),
            pltpu.VMEM((2, 3, 16, 1792), bf16),
            pltpu.VMEM((4, 8, 1792), f32),
            dma((2, 7)), dma((2, 7)),
            dma((2, 5, 4)), dma((2, 5, 4)),
            dma((2, 2, 3)), dma((2, 2, 3)),
            dma((7,)), dma((7,)),
            dma((4,)),
        ],
        compiler_params=pltpu.CompilerParams(
            collective_id=0, has_side_effects=True, vmem_limit_bytes=56 << 20
        ),
    )(served, served_far, queries, row_slots, w_uv, w_out, residual, w_down)


def serve_kernel(group_passages, passage_place, latents, served, served_far, sem):
    s, e = lax.axis_index("store"), lax.axis_index("ep")
    y, z = e // 4, e % 4
    copies = []
    for g in range(8):
        def piece(j, q, dst, i):
            place = passage_place[group_passages[g * 32 + s * 4 + j]] - s * 32
            copy = pltpu.make_async_copy(
                latents.at[place, pl.ds(pl.multiple_of(q * 144, 16), 144)], dst, sem.at[g, i]
            )
            copy.start()
            copies.append(copy)

        piece(y, z, served.at[g], 4)
        for i in range(4):
            piece(
                jnp.where(s < 4, i, lax.rem(y + 2, 4)), jnp.where(s < 4, lax.rem(z + 2, 4), i),
                served_far.at[g, i], i,
            )
    for copy in copies:
        copy.wait()


def serve(latent_store, group_passages, passage_place):
    smem = pl.BlockSpec(memory_space=pltpu.SMEM)
    vmem = pl.BlockSpec(memory_space=pltpu.VMEM)
    anywhere = pl.BlockSpec(memory_space=pl.ANY)
    return pl.pallas_call(
        serve_kernel,
        name="serve",
        out_shape=(
            jax.ShapeDtypeStruct((8, 144, 128), jnp.bfloat16),
            jax.ShapeDtypeStruct((8, 4, 144, 128), jnp.bfloat16),
        ),
        in_specs=[smem, smem, anywhere],
        out_specs=(vmem, vmem),
        scratch_shapes=[pltpu.SemaphoreType.DMA((8, 5))],
    )(group_passages, passage_place, jnp.swapaxes(latent_store, 1, 2))


def front(queries, residual_in, latent_store, group_passages, row_slots, passage_place, w_uv, w_out, w_down):
    served, served_far = serve(latent_store, group_passages, passage_place)
    return attend_call(served, served_far, queries, row_slots.T, w_uv, w_out, residual_in, w_down[0])


def expert_kernel(
    normed, mixed, place, weigh, w_gate, w_up, down_cols,
    out,
    outgoing, arrived, x_rows, w_in, w_down, pre, hid, y_part, y_rows, back, returned,
    t_send, t_recv, a_send, a_recv, h_send, h_recv, y_send, y_recv, b_send, b_recv, w_sem,
):
    s = lax.axis_index("store")
    e = lax.axis_index("ep")
    y, z = e // 4, e % 4
    sibling = s + 1 - 2 * (s % 2)

    def on_store(d):
        return lax.rem(s + d, 8)

    def on_ep(dy, dz):
        return lax.rem(y + dy, 4) * 4 + lax.rem(z + dz, 4)

    barrier = pltpu.get_barrier_semaphore()
    peers = [(on_store(d), e) for d in range(1, 8)]
    peers += [(s, on_ep(dy, dz)) for dy in range(4) for dz in range(4) if dy or dz]
    for peer in peers:
        pl.semaphore_signal(barrier, inc=1, device_id=peer, device_id_type=MESH)
    loads = [
        pltpu.make_async_copy(w_gate, w_in.at[:, 0:256], w_sem.at[0]),
        pltpu.make_async_copy(w_up, w_in.at[:, 256:512], w_sem.at[1]),
        pltpu.make_async_copy(down_cols, w_down, w_sem.at[2]),
    ]
    for load in loads:
        load.start()
    outgoing[...] = jnp.dot(
        place[...], normed[...], preferred_element_type=jnp.float32
    ).astype(jnp.bfloat16).reshape(16, 16, 1792)
    pl.semaphore_wait(barrier, len(peers))

    def copy_to(src, dst, send, recv, device):
        return pltpu.make_async_remote_copy(
            src_ref=src, dst_ref=dst, send_sem=send, recv_sem=recv, device_id=device, device_id_type=MESH
        )

    def dispatch(k, dz):
        to = on_ep(offset_of(k), dz)
        return copy_to(outgoing.at[to], arrived.at[e], t_send.at[k, dz], t_recv.at[k, dz], (s, to))

    def give_back(k, dz):
        to = on_ep(4 - offset_of(k), dz)
        return copy_to(back.at[k, lax.rem(z + dz, 4)], returned.at[e], b_send.at[k, dz], b_recv.at[k, dz], (s, to))

    def gather(k, kind):
        to = {0: 2, 1: 6, 2: 2, 3: 6}.get(kind)
        to = sibling if to is None else on_store(to)
        block = on_store((0, 0, 6, 2, 0, 6, 2, 4, 4)[kind])
        low = pl.multiple_of(block * 16, 16)
        columns = {2: (0, 3584), 3: (3584, 3584), 7: (0, 3584), 8: (3584, 3584)}.get(kind, (0, 7168))
        ref = x_rows.at[k, pl.ds(low, 16), pl.ds(*columns)]
        return copy_to(ref, ref, a_send.at[k, kind], a_recv.at[k, kind], (to, e))

    def share(k, kind):
        to = on_store((2, 6, 4)[kind]) if kind < 3 else sibling
        block = on_store((0, 0, 0, 0, 6, 2, 4)[kind])
        ref = hid.at[k, :, pl.ds(pl.multiple_of(block * 256, 256), 256)]
        return copy_to(ref, ref, h_send.at[k, kind], h_recv.at[k, kind], (to, e))

    def hand_over(k, d):
        to = on_store(d)
        return copy_to(
            y_part.at[k, pl.ds(pl.multiple_of(to * 16, 16), 16)],
            y_rows.at[k, :, pl.ds(pl.multiple_of(s * 896, 896), 896)],
            y_send.at[k, d - 1], y_recv.at[k, d - 1], (to, e),
        )

    for k in range(4):
        for dz in (0, 1, 3, 2):
            if k or dz:
                dispatch(k, dz).start()
    arrived[e] = outgoing[e]

    rows16 = lax.broadcasted_iota(jnp.int32, (16, 64), 0)
    cols64 = lax.broadcasted_iota(jnp.int32, (16, 64), 1)
    rows64 = lax.broadcasted_iota(jnp.int32, (64, 16), 0)
    cols16 = lax.broadcasted_iota(jnp.int32, (64, 16), 1)

    def take(q):
        return (cols64 == (rows16 // 4) * 16 + q * 4 + rows16 % 4).astype(jnp.bfloat16)

    def put(q):
        return (rows64 == (cols16 // 4) * 16 + q * 4 + cols16 % 4).astype(jnp.bfloat16)

    def enter(k):
        for dz in range(1, 4):
            dispatch(k, dz).wait_recv()

        @pl.when(k > 0)
        def _():
            dispatch(k, 0).wait_recv()

        line = lax.rem(y + 4 - offset_of(k), 4)
        block = arrived[pl.ds(line * 4, 4)].reshape(64, 1792)
        for q in range(4):
            x_rows[k, pl.ds(pl.multiple_of(s * 16, 16), 16), q * 1792:(q + 1) * 1792] = jnp.dot(
                take(q), block, preferred_element_type=jnp.float32
            ).astype(jnp.bfloat16)
        for kind in (0, 1, 4):
            gather(k, kind).start()

    def pass_on(k):
        for kind in (0, 1):
            gather(k, kind).wait_recv()
            gather(k, kind + 2).start()
            gather(k, kind + 5).start()

    def hidden(k):
        for kind in (2, 3):
            gather(k, kind).wait_recv()
            gather(k, kind + 5).start()
        for kind in range(4, 9):
            gather(k, kind).wait_recv()
        pre[...] = jnp.zeros_like(pre)

        def add(q, _):
            low = pl.multiple_of(q * 1792, 1792)
            pre[...] += jnp.dot(
                x_rows[k, :, pl.ds(low, 1792)], w_in[pl.ds(low, 1792)], preferred_element_type=jnp.float32
            )
            return 0

        lax.fori_loop(0, 4, add, 0)
        gate = pre[:, 0:256]
        hid[k, :, pl.ds(pl.multiple_of(s * 256, 256), 256)] = (
            gate / (1.0 + jnp.exp(-gate)) * pre[:, 256:512]
        ).astype(jnp.bfloat16)
        for kind in range(4):
            share(k, kind).start()

    def project(k):
        for kind in range(3):
            share(k, kind).wait_recv()
            share(k, kind + 4).start()
        for kind in range(3, 7):
            share(k, kind).wait_recv()
        y_part[k] = jnp.dot(hid[k], w_down[...], preferred_element_type=jnp.float32).astype(jnp.bfloat16)
        for d in range(1, 8):
            hand_over(k, d).start()
        y_rows[k, :, pl.ds(pl.multiple_of(s * 896, 896), 896)] = y_part[k, pl.ds(pl.multiple_of(s * 16, 16), 16)]

    def leave(k):
        for d in range(1, 8):
            hand_over(k, d).wait_recv()
        total = jnp.zeros((64, 1792), jnp.float32)
        for q in range(4):
            total = total + jnp.dot(
                put(q), y_rows[k, :, q * 1792:(q + 1) * 1792], preferred_element_type=jnp.float32
            )
        back[k] = total.astype(jnp.bfloat16).reshape(4, 16, 1792)
        for dz in range(1, 4):
            give_back(k, dz).start()

        @pl.when(k > 0)
        def _():
            give_back(k, 0).start()

        @pl.when(k == 0)
        def _():
            returned[e] = back[k, z]

    def step(t, _):
        @pl.when(t < 4)
        def _():
            enter(t)

        @pl.when(t == 1)
        def _():
            for load in loads:
                load.wait()

        @pl.when((t >= 1) & (t < 5))
        def _():
            hidden(t - 1)

        @pl.when(t < 4)
        def _():
            pass_on(t)

        @pl.when((t >= 2) & (t < 6))
        def _():
            project(t - 2)

        @pl.when(t >= 3)
        def _():
            leave(t - 3)

        return 0

    lax.fori_loop(0, 7, step, 0)

    for k in range(4):
        for dz in range(4):
            if k or dz:
                give_back(k, dz).wait_recv()
    rows = returned[...].reshape(256, 1792)
    total = jnp.dot(weigh[0], rows, preferred_element_type=jnp.float32) + jnp.dot(
        weigh[1], rows, preferred_element_type=jnp.float32
    )
    for q in range(4):
        out[:, q * 1792:(q + 1) * 1792] = (
            mixed[:, q * 1792:(q + 1) * 1792] + total[q * 8:(q + 1) * 8]
        ).astype(jnp.bfloat16)

    for k in range(4):
        for dz in range(4):
            if k or dz:
                dispatch(k, dz).wait_send()
                give_back(k, dz).wait_send()
        for kind in range(9):
            gather(k, kind).wait_send()
        for kind in range(7):
            share(k, kind).wait_send()
            hand_over(k, kind + 1).wait_send()


def expert_call(normed, mixed, place, weigh, w_gate, w_up, down_cols):
    vmem = pl.BlockSpec(memory_space=pltpu.VMEM)
    anywhere = pl.BlockSpec(memory_space=pl.ANY)
    bf16, f32 = jnp.bfloat16, jnp.float32
    dma = pltpu.SemaphoreType.DMA
    return pl.pallas_call(
        expert_kernel,
        name="experts",
        out_shape=jax.ShapeDtypeStruct((8, 7168), bf16),
        in_specs=[vmem, vmem, vmem, vmem, anywhere, anywhere, anywhere],
        out_specs=vmem,
        scratch_shapes=[
            pltpu.VMEM((16, 16, 1792), bf16),
            pltpu.VMEM((16, 16, 1792), bf16),
            pltpu.VMEM((4, 128, 7168), bf16),
            pltpu.VMEM((7168, 512), bf16),
            pltpu.VMEM((2048, 896), bf16),
            pltpu.VMEM((128, 512), f32),
            pltpu.VMEM((4, 128, 2048), bf16),
            pltpu.VMEM((4, 128, 896), bf16),
            pltpu.VMEM((4, 16, 7168), bf16),
            pltpu.VMEM((4, 4, 16, 1792), bf16),
            pltpu.VMEM((16, 16, 1792), bf16),
            dma((4, 4)), dma((4, 4)),
            dma((4, 9)), dma((4, 9)),
            dma((4, 7)), dma((4, 7)),
            dma((4, 7)), dma((4, 7)),
            dma((4, 4)), dma((4, 4)),
            dma((3,)),
        ],
        compiler_params=pltpu.CompilerParams(
            collective_id=1, has_side_effects=True, vmem_limit_bytes=56 << 20
        ),
    )(normed, mixed, place, weigh, w_gate, w_up, down_cols)


def routing(expert_ids, expert_gates):
    experts = jnp.arange(16, dtype=jnp.int32)
    named = (expert_ids[:, :, None] == experts).astype(jnp.float32)
    routed = jnp.sum(named, axis=1)
    gate = jnp.sum(named * expert_gates[:, :, None], axis=1)
    earlier = jnp.cumsum(routed, axis=0) - routed
    depth = jnp.arange(4, dtype=jnp.float32)
    slot = jnp.where((routed[..., None] > 0.5) & (earlier[..., None] == depth), 1.0, 0.0)
    eye = jnp.eye(4, dtype=jnp.float32)
    place = jnp.einsum("rec,qp->eqcpr", slot, eye).reshape(256, 32).astype(jnp.bfloat16)
    held = slot * gate[..., None]
    high = held.astype(jnp.bfloat16)
    low = (held - high.astype(jnp.float32)).astype(jnp.bfloat16)
    weigh = jnp.stack([high, low]).astype(jnp.float32)
    weigh = jnp.einsum("nrec,qp->nqrepc", weigh, eye).reshape(2, 32, 256).astype(jnp.bfloat16)
    return place, weigh


def body(
    queries, residual_in, latent_store, group_passages, row_slots, passage_place, w_uv, w_out,
    expert_ids, expert_gates, w_gate, w_up, w_down,
):
    mixed, normed, down_cols = front(
        queries, residual_in, latent_store, group_passages, row_slots, passage_place, w_uv, w_out, w_down
    )
    place, weigh = routing(expert_ids, expert_gates)
    return expert_call(normed, mixed, place, weigh, w_gate[0], w_up[0], down_cols)


def solution(mesh):
    return jax.shard_map(
        body,
        mesh=mesh,
        in_specs=(
            P("store", "ep"),
            P(("store", "ep"), None),
            P("store", None, None),
            P(),
            P("store", None),
            P(),
            P("ep", None, None),
            P("ep", None),
            P(("store", "ep"), None),
            P(("store", "ep"), None),
            P("ep", None, "store"),
            P("ep", None, "store"),
            P("ep", "store", None),
        ),
        out_specs=P(("store", "ep"), None),
        check_vma=False,
    )
```

```python
import functools

import jax
import jax.numpy as jnp
from jax import lax
from jax.experimental import pallas as pl
from jax.experimental.pallas import tpu as pltpu
from jax.sharding import PartitionSpec as P

SCALE = 192.0 ** (-0.5) * 1.4426950408889634
MESH = pl.DeviceIdType.MESH
LOW = -1e29
FAR_LOW = 1e30


def offset_of(i):
    return i + i // 2 - 2 * (i // 3)


def layer_kernel(
    served, served_far, queries, row_slots, w_uv, w_out, residual, ids, gates, w_gate, w_up, w_down,
    out,
    kv, heads, mask, top, total, acc, head_out, out_w, part, part_in, summed, summed_in, rows,
    table, weigh, normed, outgoing, arrived, x_rows, in_w, down_w, pre, hid, y_part, returned, mix_out, mix_in,
    x_send, x_recv, g_send, g_recv, r_send, r_recv, d_send, d_recv, w_sem,
    n_send, n_recv, t_send, t_recv, a_send, a_recv, h_send, h_recv, b_send, b_recv, m_send, m_recv,
):
    s = lax.axis_index("store")
    e = lax.axis_index("ep")
    y, z = e // 4, e % 4

    def at_y(d):
        return (s, lax.rem(y + d, 4) * 4 + z)

    def at_z(d):
        return (s, y * 4 + lax.rem(z + d, 4))

    def at_s(d):
        return (lax.rem(s + d, 8), e)

    def quarter(q):
        return pl.ds(pl.multiple_of(q * 144, 16), 144)

    sibling = s + 1 - 2 * (s % 2)

    def on_ep(dy, dz):
        return lax.rem(y + dy, 4) * 4 + lax.rem(z + dz, 4)

    peers = [at_s(d) for d in range(1, 8)]
    peers += [(s, on_ep(dy, dz)) for dy in range(4) for dz in range(4) if dy or dz]
    barrier = pltpu.get_barrier_semaphore()
    for peer in peers:
        pl.semaphore_signal(barrier, inc=1, device_id=peer, device_id_type=MESH)
    get_w = pltpu.make_async_copy(w_out, out_w, w_sem.at[0])
    get_in = [
        pltpu.make_async_copy(w_gate, in_w.at[:, 0:256], w_sem.at[4]),
        pltpu.make_async_copy(w_up, in_w.at[:, 256:512], w_sem.at[5]),
    ]
    for load in [get_w] + get_in:
        load.start()

    lane_row = lax.broadcasted_iota(jnp.int32, (8, 128), 1) % 8
    repeat = (lax.broadcasted_iota(jnp.int32, (8, 128), 0) == lane_row).astype(jnp.float32)
    wide_ids = jnp.dot(ids[...].astype(jnp.float32), repeat, preferred_element_type=jnp.float32)
    wide_gates = jnp.dot(
        gates[...], repeat, preferred_element_type=jnp.float32, precision=lax.Precision.HIGHEST
    )
    pair = lax.broadcasted_iota(jnp.int32, (64, 128), 0)
    expert = (pair // 4).astype(jnp.float32)
    routed = jnp.zeros((64, 128), jnp.float32)
    gate = jnp.zeros((64, 128), jnp.float32)
    for i in range(4):
        named = (wide_ids[i:i + 1] == expert).astype(jnp.float32)
        routed = routed + named
        gate = gate + named * wide_gates[i:i + 1]
    before = lax.broadcasted_iota(jnp.int32, (128, 128), 0)
    upto = lax.broadcasted_iota(jnp.int32, (128, 128), 1) % 8
    earlier = jnp.dot(
        routed.astype(jnp.bfloat16), (before < upto).astype(jnp.bfloat16), preferred_element_type=jnp.float32
    )
    table[s] = jnp.where((routed > 0.5) & (earlier == (pair % 4).astype(jnp.float32)), gate, 0.0)
    pl.semaphore_wait(barrier, len(peers))

    sent = []
    for d in range(1, 8):
        to = at_s(d)
        copy = pltpu.make_async_remote_copy(
            src_ref=served.at[to[0]], dst_ref=kv.at[y, s, quarter(z)],
            send_sem=x_send.at[0, d - 1], recv_sem=x_recv.at[0, d - 1],
            device_id=to, device_id_type=MESH,
        )
        copy.start()
        sent.append(copy)
    keep = pltpu.make_async_copy(served.at[s], kv.at[y, s, quarter(z)], w_sem.at[2])
    keep.start()

    def copy_to(src, dst, send, recv, device):
        return pltpu.make_async_remote_copy(
            src_ref=src, dst_ref=dst, send_sem=send, recv_sem=recv, device_id=device, device_id_type=MESH
        )

    def far_copies(whole):
        def target(ref):
            return ref.at[lax.rem(y + 2, 4), s] if whole else ref.at[:, s, quarter(lax.rem(z + 2, 4))]

        def source(g):
            return served_far.at[g].reshape(576, 128) if whole else served_far.at[g]

        return [
            pltpu.make_async_remote_copy(
                src_ref=source(at_s(d)[0]), dst_ref=target(kv),
                send_sem=x_send.at[1, d - 1], recv_sem=x_recv.at[1, d - 1],
                device_id=at_s(d), device_id_type=MESH,
            )
            for d in range(1, 8)
        ] + [pltpu.make_async_copy(source(s), target(kv), w_sem.at[3])]

    def each_far(act):
        for whole in (False, True):
            @pl.when((s >= 4) if whole else (s < 4))
            def _():
                for copy in far_copies(whole):
                    act(copy)

    for h in range(4):
        heads[h * 128:(h + 1) * 128] = queries[:, h * 576:(h + 1) * 576]
    slot = lax.broadcasted_iota(jnp.int32, (32, 128), 0)
    chosen = jnp.zeros((32, 128), jnp.bool_)
    for i in range(16):
        chosen = chosen | (row_slots[i:i + 1] == slot)
    chosen = chosen.astype(jnp.bfloat16)
    slot_row = lax.broadcasted_iota(jnp.int32, (32, 512), 0)
    token_col = lax.broadcasted_iota(jnp.int32, (32, 512), 1)
    for j in range(4):
        for half in (0, 1):
            spread = (slot_row == (token_col // 128 + 4 * half) * 4 + j).astype(jnp.bfloat16)
            live = lax.dot_general(
                chosen, spread, (((0,), (0,)), ((), ())), preferred_element_type=jnp.float32
            )
            mask[j, half] = (live - 1.0) * FAR_LOW
    top[...] = jnp.full_like(top, LOW)
    total[...] = jnp.zeros_like(total)
    acc[...] = jnp.zeros_like(acc)

    def chunk(half, first, second):
        dy, dz = (first, second) if half == 0 else (second, first)
        return lax.rem(y - dy + 4, 4), lax.rem(z - dz + 4, 4)

    def attend(j, half):
        keys = jnp.concatenate([kv[j, half * 4 + i] for i in range(4)], axis=1)
        scores = jnp.dot(heads[...], keys, preferred_element_type=jnp.float32) * SCALE
        scores = (scores.reshape(4, 128, 512) + mask[j, half]).reshape(512, 512)
        old = top[...]
        new = jnp.maximum(old, jnp.max(scores, axis=1, keepdims=True))
        exponent = jnp.exp2(scores - new[:, 0:1])
        scale = jnp.exp2(old - new)
        top[...] = new
        total[...] = total[...] * scale + jnp.sum(exponent, axis=1, keepdims=True)
        acc[...] = acc[...] * scale[:, 0:1] + lax.dot_general(
            exponent.astype(jnp.bfloat16), keys[0:512], (((1,), (1,)), ((), ())),
            preferred_element_type=jnp.float32,
        )

    def build_weigh():
        lane = lax.broadcasted_iota(jnp.int32, (64, 128), 1)
        gated = jnp.concatenate([jnp.where(lane // 8 == g, table[g], 0.0) for g in range(8)], axis=0)
        from_row = lax.broadcasted_iota(jnp.int32, (512, 512), 0)
        to_col = lax.broadcasted_iota(jnp.int32, (512, 512), 1)
        place = (to_col // 4 % 8) * 64 + (to_col // 32) * 4 + to_col % 4
        move = (from_row == place).astype(jnp.bfloat16)
        high = gated.astype(jnp.bfloat16)
        low = (gated - high.astype(jnp.float32)).astype(jnp.bfloat16)
        for i, held in ((0, high), (1, low)):
            weigh[i] = lax.dot_general(
                held, move, (((0,), (0,)), ((), ())), preferred_element_type=jnp.float32
            )[0:64].astype(jnp.bfloat16)

    def gather_copy(half, group, kind, place):
        low = half * 4 + (2 if kind == 3 else 0)
        size = 2 if kind >= 2 else 4
        on_y = (half == 0) == (group is None)
        to = (at_y if on_y else at_z)(1 if kind % 2 == 0 else 3)
        block = kv.at[place[0], pl.ds(low, size), quarter(place[1])]
        index = 4 if group is None else group
        return pltpu.make_async_remote_copy(
            src_ref=block, dst_ref=block,
            send_sem=g_send.at[half, index, kind], recv_sem=g_recv.at[half, index, kind],
            device_id=to, device_id_type=MESH,
        )

    def launch(group, offset):
        for half in (0, 1):
            for kind in (0, 1):
                gather_copy(half, group, kind, chunk(half, offset, 0)).start()

    keep.wait()
    for copy in sent:
        copy.wait_recv()
    launch(None, 0)
    launch(0, 0)
    tables = []
    for d in range(1, 8):
        copy = pltpu.make_async_remote_copy(
            src_ref=table.at[s], dst_ref=table.at[s], send_sem=n_send.at[d], recv_sem=n_recv.at[d],
            device_id=at_s(d), device_id_type=MESH,
        )
        copy.start()
        tables.append(copy)
    each_far(lambda copy: copy.start())
    keep_w = pltpu.make_async_copy(
        w_down.at[:, pl.ds(pl.multiple_of(s * 896, 896), 896)],
        down_w.at[pl.ds(pl.multiple_of(s * 256, 256), 256)], w_sem.at[1],
    )
    keep_w.start()
    moved = []
    for d in range(1, 8):
        to = at_s(d)
        copy = pltpu.make_async_remote_copy(
            src_ref=w_down.at[:, pl.ds(pl.multiple_of(to[0] * 896, 896), 896)],
            dst_ref=down_w.at[pl.ds(pl.multiple_of(s * 256, 256), 256)],
            send_sem=d_send.at[d - 1], recv_sem=d_recv.at[d - 1],
            device_id=to, device_id_type=MESH,
        )
        copy.start()
        moved.append(copy)
    for kind in (0, 1):
        offset = 1 if kind == 0 else 3
        for half in (0, 1):
            gather_copy(half, None, kind, (y, z)).wait_recv()
            gather_copy(half, None, kind + 2, chunk(half, offset, 0)).start()
        launch(kind + 1, offset)
    for half in (0, 1):
        for kind in (2, 3):
            gather_copy(half, None, kind, (y, z)).wait_recv()
    launch(3, 2)
    for copy in tables:
        copy.wait_recv()
    build_weigh()
    attend(y, 1)

    def take_far(copy):
        if copy.is_remote:
            copy.wait_recv()
        else:
            copy.wait()

    each_far(take_far)
    attend(lax.rem(y + 2, 4), 1)

    def sides(i, _):
        for kind in (0, 1):
            for half in (0, 1):
                gather_copy(half, i, kind, (y, z)).wait_recv()
        attend(chunk(0, offset_of(i), 0)[0], 0)
        return 0

    lax.fori_loop(0, 4, sides, 0)

    def last(i, _):
        attend(lax.rem(y + 1 + 2 * i, 4), 1)
        return 0

    lax.fori_loop(0, 2, last, 0)

    for h in range(4):
        own = pl.ds(h * 128, 128)
        latent = (acc[own] / total[own, 0:1]).astype(jnp.bfloat16)
        head_out[:, h * 128:(h + 1) * 128] = jnp.dot(
            latent, w_uv[h], preferred_element_type=jnp.float32
        ).astype(jnp.bfloat16)
    get_w.wait()

    first = []
    for half in (0, 1):
        def project(t, _):
            lane = pl.multiple_of(t * 256, 256)
            both = []
            for k in (0, 1):
                column = pl.multiple_of(half * 3584 + k * 1792 + t * 256, 256)
                both.append(jnp.dot(
                    head_out[...], out_w[:, pl.ds(column, 256)], preferred_element_type=jnp.float32
                ).reshape(16, 8, 256))
            tile = jnp.concatenate(both, axis=1).astype(jnp.bfloat16)
            if half == 0:
                part[0, :, :, pl.ds(lane, 256)] = tile
            else:
                for p in range(16):
                    part[1, (p % 4) * 4 + p // 4, :, pl.ds(lane, 256)] = tile[p]
            return 0

        lax.fori_loop(0, 7, project, 0)
        for d in (1, 2, 3):
            to, line = (at_y(d), lax.rem(y + d, 4)) if half == 0 else (at_z(d), lax.rem(z + d, 4))
            copy = pltpu.make_async_remote_copy(
                src_ref=part.at[half, pl.ds(line * 4, 4)], dst_ref=part_in.at[half, d - 1],
                send_sem=r_send.at[half, 0, d - 1], recv_sem=r_recv.at[half, 0, d - 1],
                device_id=to, device_id_type=MESH,
            )
            copy.start()
            first.append(copy)
    second = []
    for half in (0, 1):
        for d in (1, 2, 3):
            first[half * 3 + d - 1].wait_recv()
        own = y if half == 0 else z

        def add(k, _):
            value = part[half, own * 4 + k].astype(jnp.float32)
            for d in range(3):
                value = value + part_in[half, d, k].astype(jnp.float32)
            summed[half, k] = value.astype(jnp.bfloat16)
            return 0

        lax.fori_loop(0, 4, add, 0)
        for d in (1, 2, 3):
            to, line = (at_z(d), lax.rem(z + d, 4)) if half == 0 else (at_y(d), lax.rem(y + d, 4))
            copy = pltpu.make_async_remote_copy(
                src_ref=summed.at[half, line], dst_ref=summed_in.at[half, d - 1],
                send_sem=r_send.at[half, 1, d - 1], recv_sem=r_recv.at[half, 1, d - 1],
                device_id=to, device_id_type=MESH,
            )
            copy.start()
            second.append(copy)
    squares = jnp.zeros((8, 1), jnp.float32)
    for half in (0, 1):
        for d in (1, 2, 3):
            second[half * 3 + d - 1].wait_recv()
        value = summed[half, z if half == 0 else y].astype(jnp.float32)
        for d in range(3):
            value = value + summed_in[half, d].astype(jnp.float32)
        for k in (0, 1):
            q = 2 * half + k
            row = residual[:, q * 1792:(q + 1) * 1792].astype(jnp.float32) + value[k * 8:(k + 1) * 8]
            rows[q] = row
            squares = squares + jnp.sum(row * row, axis=1, keepdims=True)
    norm = lax.rsqrt(squares / 7168.0 + 1e-06)
    for q in (0, 2):
        two = jnp.concatenate([rows[q] * norm, rows[q + 1] * norm], axis=0)
        normed[0, q * 8:(q + 2) * 8] = two.astype(jnp.bfloat16)

    swap = copy_to(normed.at[0], normed.at[1], n_send.at[0], n_recv.at[0], at_s(4))
    swap.start()

    def dispatch(side, k, dz):
        to = on_ep(offset_of(k), dz)
        return copy_to(
            outgoing.at[side, to], arrived.at[side, e], t_send.at[side, k, dz], t_recv.at[side, k, dz], (s, to)
        )

    def give_back(k, dz):
        to = on_ep(4 - offset_of(k), dz)
        return copy_to(y_part.at[k, lax.rem(z + dz, 4)], returned.at[e], b_send.at[k, dz], b_recv.at[k, dz], (s, to))

    def gather(k, kind):
        to = at_s((2, 6)[kind]) if kind < 2 else (sibling, e)
        block = lax.rem(s + (0, 0, 0, 4, 6, 2)[kind], 8)
        ref = x_rows.at[k, pl.ds(pl.multiple_of(block * 16, 16), 16)]
        return copy_to(ref, ref, a_send.at[k, kind], a_recv.at[k, kind], to)

    def share(k, kind):
        to = at_s((2, 6, 4)[kind]) if kind < 3 else (sibling, e)
        block = lax.rem(s + (0, 0, 0, 0, 6, 2, 4)[kind], 8)
        ref = hid.at[k, :, pl.ds(pl.multiple_of(block * 256, 256), 256)]
        return copy_to(ref, ref, h_send.at[k, kind], h_recv.at[k, kind], to)

    def spread_rows(side):
        group = lax.rem(s + 4 * side, 8)
        to_row = lax.broadcasted_iota(jnp.int32, (256, 64), 0)
        from_pair = lax.broadcasted_iota(jnp.int32, (256, 64), 1)
        widen = (from_pair == (to_row // 16) * 4 + to_row % 4).astype(jnp.bfloat16)
        held = jnp.dot(
            widen, (table[group] > 0).astype(jnp.bfloat16), preferred_element_type=jnp.float32
        )[:, 0:32]
        row_quarter = lax.broadcasted_iota(jnp.int32, (256, 32), 0) // 4 % 4
        col_quarter = lax.broadcasted_iota(jnp.int32, (256, 32), 1) // 8
        place = jnp.where(row_quarter == col_quarter, held, 0.0).astype(jnp.bfloat16)
        outgoing[side] = jnp.dot(
            place, normed[side], preferred_element_type=jnp.float32
        ).astype(jnp.bfloat16).reshape(16, 16, 1792)
        arrived[side, e] = outgoing[side, e]

    def send_rows(side, k):
        for dz in (0, 1, 3, 2):
            if k or dz:
                dispatch(side, k, dz).start()

    spread_rows(0)
    send_rows(0, 0)
    send_rows(0, 1)
    swap.wait_recv()
    spread_rows(1)
    for side, k in ((1, 0), (0, 2), (1, 1), (0, 3), (1, 2), (1, 3)):
        send_rows(side, k)

    rows16 = lax.broadcasted_iota(jnp.int32, (16, 64), 0)
    cols64 = lax.broadcasted_iota(jnp.int32, (16, 64), 1)

    def enter(side, k):
        for dz in range(1, 4):
            dispatch(side, k, dz).wait_recv()

        @pl.when(k > 0)
        def _():
            dispatch(side, k, 0).wait_recv()

        line = lax.rem(y + 4 - offset_of(k), 4)
        block = arrived[side, pl.ds(line * 4, 4)].reshape(64, 1792)
        low = pl.multiple_of(lax.rem(s + 4 * side, 8) * 16, 16)
        for q in range(4):
            take = (cols64 == (rows16 // 4) * 16 + q * 4 + rows16 % 4).astype(jnp.bfloat16)
            x_rows[k, pl.ds(low, 16), q * 1792:(q + 1) * 1792] = jnp.dot(
                take, block, preferred_element_type=jnp.float32
            ).astype(jnp.bfloat16)
        for kind in ((0, 1, 2), (3,))[side]:
            gather(k, kind).start()

    def pass_on(k):
        for kind in (0, 1):
            gather(k, kind).wait_recv()
            gather(k, kind + 4).start()

    def hidden(k):
        for kind in range(2, 6):
            gather(k, kind).wait_recv()
        pre[...] = jnp.zeros_like(pre)

        def add(q, _):
            low = pl.multiple_of(q * 1792, 1792)
            pre[...] += jnp.dot(
                x_rows[k, :, pl.ds(low, 1792)], in_w[pl.ds(low, 1792)], preferred_element_type=jnp.float32
            )
            return 0

        lax.fori_loop(0, 4, add, 0)
        gate = pre[:, 0:256]
        hid[k, :, pl.ds(pl.multiple_of(s * 256, 256), 256)] = (
            gate / (1.0 + jnp.exp(-gate)) * pre[:, 256:512]
        ).astype(jnp.bfloat16)
        for kind in range(4):
            share(k, kind).start()

    to128 = lax.broadcasted_iota(jnp.int32, (128, 128), 0)
    from128 = lax.broadcasted_iota(jnp.int32, (128, 128), 1)

    def project(k):
        for kind in range(3):
            share(k, kind).wait_recv()
            share(k, kind + 4).start()
        for kind in range(3, 7):
            share(k, kind).wait_recv()
        value = jnp.dot(hid[k], down_w[...], preferred_element_type=jnp.float32).astype(jnp.bfloat16)
        order = (from128 == (to128 // 4 % 8) * 16 + (to128 // 32) * 4 + to128 % 4).astype(jnp.bfloat16)
        y_part[k] = jnp.dot(order, value, preferred_element_type=jnp.float32).astype(jnp.bfloat16).reshape(4, 32, 896)
        for dz in range(1, 4):
            give_back(k, dz).start()

        @pl.when(k > 0)
        def _():
            give_back(k, 0).start()

        @pl.when(k == 0)
        def _():
            returned[e] = y_part[k, z]

    def step(t, _):
        @pl.when(t < 4)
        def _():
            enter(0, t)

        @pl.when(t == 1)
        def _():
            for load in get_in:
                load.wait()

        @pl.when((t >= 1) & (t < 5))
        def _():
            hidden(t - 1)

        @pl.when(t < 4)
        def _():
            enter(1, t)
            pass_on(t)

        @pl.when(t == 2)
        def _():
            keep_w.wait()
            for copy in moved:
                copy.wait_recv()

        @pl.when(t >= 2)
        def _():
            project(t - 2)

        return 0

    lax.fori_loop(0, 6, step, 0)

    for k in range(4):
        for dz in range(4):
            if k or dz:
                give_back(k, dz).wait_recv()
    back = returned[...].reshape(512, 896)
    mix_out[...] = jnp.dot(weigh[0], back, preferred_element_type=jnp.float32) + jnp.dot(
        weigh[1], back, preferred_element_type=jnp.float32
    )
    columns = pl.ds(pl.multiple_of(s * 896, 896), 896)
    handed = []
    for d in (4, 2, 6, 3, 5, 1, 7):
        to = at_s(d)
        copy = copy_to(
            mix_out.at[pl.ds(pl.multiple_of(to[0] * 8, 8), 8)], mix_in.at[:, columns],
            m_send.at[d - 1], m_recv.at[d - 1], to,
        )
        copy.start()
        handed.append(copy)
    mix_in[:, columns] = mix_out[pl.ds(pl.multiple_of(s * 8, 8), 8)]
    for copy in handed:
        copy.wait_recv()
    for q in range(4):
        own = slice(q * 1792, (q + 1) * 1792)
        out[:, own] = (rows[q] + mix_in[:, own]).astype(jnp.bfloat16)

    for copy in handed + tables + [swap] + moved:
        copy.wait_send()
    for k in range(4):
        for dz in range(4):
            if k or dz:
                dispatch(0, k, dz).wait_send()
                dispatch(1, k, dz).wait_send()
                give_back(k, dz).wait_send()
        for kind in range(6):
            gather(k, kind).wait_send()
        for kind in range(7):
            share(k, kind).wait_send()
    for copy in sent + first + second:
        copy.wait_send()
    each_far(lambda copy: copy.wait_send() if copy.is_remote else None)
    for half in (0, 1):
        for group in range(5):
            for kind in range(4 if group == 4 else 2):
                gather_copy(half, group if group < 4 else None, kind, (y, z)).wait_send()


def layer_call(*arrays):
    vmem = pl.BlockSpec(memory_space=pltpu.VMEM)
    anywhere = pl.BlockSpec(memory_space=pl.ANY)
    bf16, f32 = jnp.bfloat16, jnp.float32
    dma = pltpu.SemaphoreType.DMA
    return pl.pallas_call(
        layer_kernel,
        name="layer",
        out_shape=jax.ShapeDtypeStruct((8, 7168), bf16),
        in_specs=[anywhere, anywhere, vmem, vmem, vmem, anywhere, vmem, vmem, vmem, anywhere, anywhere, anywhere],
        out_specs=vmem,
        scratch_shapes=[
            pltpu.VMEM((4, 8, 576, 128), bf16),
            pltpu.VMEM((512, 576), bf16),
            pltpu.VMEM((4, 2, 128, 512), f32),
            pltpu.VMEM((512, 128), f32),
            pltpu.VMEM((512, 128), f32),
            pltpu.VMEM((512, 512), f32),
            pltpu.VMEM((128, 512), bf16),
            pltpu.VMEM((512, 7168), bf16),
            pltpu.VMEM((2, 16, 16, 1792), bf16),
            pltpu.VMEM((2, 3, 4, 16, 1792), bf16),
            pltpu.VMEM((2, 4, 16, 1792), bf16),
            pltpu.VMEM((2, 3, 16, 1792), bf16),
            pltpu.VMEM((4, 8, 1792), f32),
            pltpu.VMEM((8, 64, 128), f32),
            pltpu.VMEM((2, 64, 512), bf16),
            pltpu.VMEM((2, 32, 1792), bf16),
            pltpu.VMEM((2, 16, 16, 1792), bf16),
            pltpu.VMEM((2, 16, 16, 1792), bf16),
            pltpu.VMEM((4, 128, 7168), bf16),
            pltpu.VMEM((7168, 512), bf16),
            pltpu.VMEM((2048, 896), bf16),
            pltpu.VMEM((128, 512), f32),
            pltpu.VMEM((4, 128, 2048), bf16),
            pltpu.VMEM((4, 4, 32, 896), bf16),
            pltpu.VMEM((16, 32, 896), bf16),
            pltpu.VMEM((64, 896), f32),
            pltpu.VMEM((8, 7168), f32),
            dma((2, 7)), dma((2, 7)),
            dma((2, 5, 4)), dma((2, 5, 4)),
            dma((2, 2, 3)), dma((2, 2, 3)),
            dma((7,)), dma((7,)),
            dma((6,)),
            dma((8,)), dma((8,)),
            dma((2, 4, 4)), dma((2, 4, 4)),
            dma((4, 6)), dma((4, 6)),
            dma((4, 7)), dma((4, 7)),
            dma((4, 4)), dma((4, 4)),
            dma((7,)), dma((7,)),
        ],
        compiler_params=pltpu.CompilerParams(
            collective_id=0, has_side_effects=True, vmem_limit_bytes=60 << 20
        ),
    )(*arrays)


def serve_kernel(group_passages, passage_place, latents, served, served_far, sem):
    s, e = lax.axis_index("store"), lax.axis_index("ep")
    y, z = e // 4, e % 4
    copies = []
    for g in range(8):
        def piece(j, q, dst, i):
            place = passage_place[group_passages[g * 32 + s * 4 + j]] - s * 32
            copy = pltpu.make_async_copy(
                latents.at[place, pl.ds(pl.multiple_of(q * 144, 16), 144)], dst, sem.at[g, i]
            )
            copy.start()
            copies.append(copy)

        piece(y, z, served.at[g], 4)
        for i in range(4):
            piece(
                jnp.where(s < 4, i, lax.rem(y + 2, 4)), jnp.where(s < 4, lax.rem(z + 2, 4), i),
                served_far.at[g, i], i,
            )
    for copy in copies:
        copy.wait()


def serve(latent_store, group_passages, passage_place):
    smem = pl.BlockSpec(memory_space=pltpu.SMEM)
    vmem = pl.BlockSpec(memory_space=pltpu.VMEM)
    anywhere = pl.BlockSpec(memory_space=pl.ANY)
    return pl.pallas_call(
        serve_kernel,
        name="serve",
        out_shape=(
            jax.ShapeDtypeStruct((8, 144, 128), jnp.bfloat16),
            jax.ShapeDtypeStruct((8, 4, 144, 128), jnp.bfloat16),
        ),
        in_specs=[smem, smem, anywhere],
        out_specs=(vmem, vmem),
        scratch_shapes=[pltpu.SemaphoreType.DMA((8, 5))],
    )(group_passages, passage_place, jnp.swapaxes(latent_store, 1, 2))


def body(
    queries, residual_in, latent_store, group_passages, row_slots, passage_place, w_uv, w_out,
    expert_ids, expert_gates, w_gate, w_up, w_down,
):
    served, served_far = serve(latent_store, group_passages, passage_place)
    return layer_call(
        served, served_far, queries, row_slots.T, w_uv, w_out, residual_in,
        expert_ids.T, expert_gates.T, w_gate[0], w_up[0], w_down[0],
    )


def solution(mesh):
    return jax.shard_map(
        body,
        mesh=mesh,
        in_specs=(
            P("store", "ep"),
            P(("store", "ep"), None),
            P("store", None, None),
            P(),
            P("store", None),
            P(),
            P("ep", None, None),
            P("ep", None),
            P(("store", "ep"), None),
            P(("store", "ep"), None),
            P("ep", None, "store"),
            P("ep", None, "store"),
            P("ep", "store", None),
        ),
        out_specs=P(("store", "ep"), None),
        check_vma=False,
    )
```

```python
import functools

import jax
import jax.numpy as jnp
from jax import lax
from jax.experimental import pallas as pl
from jax.experimental.pallas import tpu as pltpu
from jax.sharding import PartitionSpec as P

SCALE = 192.0 ** (-0.5) * 1.4426950408889634
MESH = pl.DeviceIdType.MESH
LOW = -1e29
FAR_LOW = 1e30


def offset_of(i):
    return i + i // 2 - 2 * (i // 3)


def layer_kernel(
    served, served_far, queries, row_slots, w_uv, w_out, residual, ids, gates, w_gate, w_up, w_down,
    out,
    kv, heads, mask, top, total, acc, head_out, out_w, part, part_in, summed, summed_in, rows,
    table, weigh, normed, outgoing, arrived, x_rows, in_w, down_w, pre, hid, y_part, returned, mix_out, mix_in,
    x_send, x_recv, g_send, g_recv, r_send, r_recv, d_send, d_recv, w_sem,
    n_send, n_recv, t_send, t_recv, a_send, a_recv, h_send, h_recv, b_send, b_recv, m_send, m_recv,
):
    s = lax.axis_index("store")
    e = lax.axis_index("ep")
    y, z = e // 4, e % 4

    def at_y(d):
        return (s, lax.rem(y + d, 4) * 4 + z)

    def at_z(d):
        return (s, y * 4 + lax.rem(z + d, 4))

    def at_s(d):
        return (lax.rem(s + d, 8), e)

    def quarter(q):
        return pl.ds(pl.multiple_of(q * 144, 16), 144)

    sibling = s + 1 - 2 * (s % 2)

    def on_ep(dy, dz):
        return lax.rem(y + dy, 4) * 4 + lax.rem(z + dz, 4)

    peers = [at_s(d) for d in range(1, 8)]
    peers += [(s, on_ep(dy, dz)) for dy in range(4) for dz in range(4) if dy or dz]
    barrier = pltpu.get_barrier_semaphore()
    for peer in peers:
        pl.semaphore_signal(barrier, inc=1, device_id=peer, device_id_type=MESH)
    get_w = pltpu.make_async_copy(w_out, out_w, w_sem.at[0])
    get_in = [
        pltpu.make_async_copy(w_gate, in_w.at[:, 0:256], w_sem.at[4]),
        pltpu.make_async_copy(w_up, in_w.at[:, 256:512], w_sem.at[5]),
    ]
    for load in [get_w] + get_in:
        load.start()

    lane_row = lax.broadcasted_iota(jnp.int32, (8, 128), 1) % 8
    repeat = (lax.broadcasted_iota(jnp.int32, (8, 128), 0) == lane_row).astype(jnp.float32)
    wide_ids = jnp.dot(ids[...].astype(jnp.float32), repeat, preferred_element_type=jnp.float32)
    wide_gates = jnp.dot(
        gates[...], repeat, preferred_element_type=jnp.float32, precision=lax.Precision.HIGHEST
    )
    pair = lax.broadcasted_iota(jnp.int32, (64, 128), 0)
    expert = (pair // 4).astype(jnp.float32)
    routed = jnp.zeros((64, 128), jnp.float32)
    gate = jnp.zeros((64, 128), jnp.float32)
    for i in range(4):
        named = (wide_ids[i:i + 1] == expert).astype(jnp.float32)
        routed = routed + named
        gate = gate + named * wide_gates[i:i + 1]
    before = lax.broadcasted_iota(jnp.int32, (128, 128), 0)
    upto = lax.broadcasted_iota(jnp.int32, (128, 128), 1) % 8
    earlier = jnp.dot(
        routed.astype(jnp.bfloat16), (before < upto).astype(jnp.bfloat16), preferred_element_type=jnp.float32
    )
    table[s] = jnp.where((routed > 0.5) & (earlier == (pair % 4).astype(jnp.float32)), gate, 0.0)
    pl.semaphore_wait(barrier, len(peers))

    sent = []
    for d in range(1, 8):
        to = at_s(d)
        copy = pltpu.make_async_remote_copy(
            src_ref=served.at[to[0]], dst_ref=kv.at[y, s, quarter(z)],
            send_sem=x_send.at[0, d - 1], recv_sem=x_recv.at[0, d - 1],
            device_id=to, device_id_type=MESH,
        )
        copy.start()
        sent.append(copy)
    keep = pltpu.make_async_copy(served.at[s], kv.at[y, s, quarter(z)], w_sem.at[2])
    keep.start()

    def copy_to(src, dst, send, recv, device):
        return pltpu.make_async_remote_copy(
            src_ref=src, dst_ref=dst, send_sem=send, recv_sem=recv, device_id=device, device_id_type=MESH
        )

    def far_copies(whole):
        def target(ref):
            return ref.at[lax.rem(y + 2, 4), s] if whole else ref.at[:, s, quarter(lax.rem(z + 2, 4))]

        def source(g):
            return served_far.at[g].reshape(576, 128) if whole else served_far.at[g]

        return [
            pltpu.make_async_remote_copy(
                src_ref=source(at_s(d)[0]), dst_ref=target(kv),
                send_sem=x_send.at[1, d - 1], recv_sem=x_recv.at[1, d - 1],
                device_id=at_s(d), device_id_type=MESH,
            )
            for d in range(1, 8)
        ] + [pltpu.make_async_copy(source(s), target(kv), w_sem.at[3])]

    def each_far(act):
        for whole in (False, True):
            @pl.when((s >= 4) if whole else (s < 4))
            def _():
                for copy in far_copies(whole):
                    act(copy)

    for h in range(4):
        heads[h * 128:(h + 1) * 128] = queries[:, h * 576:(h + 1) * 576]
    slot = lax.broadcasted_iota(jnp.int32, (32, 128), 0)
    chosen = jnp.zeros((32, 128), jnp.bool_)
    for i in range(16):
        chosen = chosen | (row_slots[i:i + 1] == slot)
    chosen = chosen.astype(jnp.bfloat16)
    slot_row = lax.broadcasted_iota(jnp.int32, (32, 512), 0)
    token_col = lax.broadcasted_iota(jnp.int32, (32, 512), 1)
    for j in range(4):
        for half in (0, 1):
            spread = (slot_row == (token_col // 128 + 4 * half) * 4 + j).astype(jnp.bfloat16)
            live = lax.dot_general(
                chosen, spread, (((0,), (0,)), ((), ())), preferred_element_type=jnp.float32
            )
            mask[j, half] = (live - 1.0) * FAR_LOW
    top[...] = jnp.full_like(top, LOW)
    total[...] = jnp.zeros_like(total)
    acc[...] = jnp.zeros_like(acc)

    def chunk(half, first, second):
        dy, dz = (first, second) if half == 0 else (second, first)
        return lax.rem(y - dy + 4, 4), lax.rem(z - dz + 4, 4)

    def attend(j, half):
        keys = jnp.concatenate([kv[j, half * 4 + i] for i in range(4)], axis=1)
        scores = jnp.dot(heads[...], keys, preferred_element_type=jnp.float32) * SCALE
        scores = (scores.reshape(4, 128, 512) + mask[j, half]).reshape(512, 512)
        old = top[...]
        new = jnp.maximum(old, jnp.max(scores, axis=1, keepdims=True))
        exponent = jnp.exp2(scores - new[:, 0:1])
        scale = jnp.exp2(old - new)
        top[...] = new
        total[...] = total[...] * scale + jnp.sum(exponent, axis=1, keepdims=True)
        acc[...] = acc[...] * scale[:, 0:1] + lax.dot_general(
            exponent.astype(jnp.bfloat16), keys[0:512], (((1,), (1,)), ((), ())),
            preferred_element_type=jnp.float32,
        )

    def build_weigh():
        lane = lax.broadcasted_iota(jnp.int32, (64, 128), 1)
        gated = jnp.concatenate([jnp.where(lane // 8 == g, table[g], 0.0) for g in range(8)], axis=0)
        from_row = lax.broadcasted_iota(jnp.int32, (512, 512), 0)
        to_col = lax.broadcasted_iota(jnp.int32, (512, 512), 1)
        place = (to_col // 4 % 8) * 64 + (to_col // 32) * 4 + to_col % 4
        move = (from_row == place).astype(jnp.bfloat16)
        high = gated.astype(jnp.bfloat16)
        low = (gated - high.astype(jnp.float32)).astype(jnp.bfloat16)
        for i, held in ((0, high), (1, low)):
            weigh[i] = lax.dot_general(
                held, move, (((0,), (0,)), ((), ())), preferred_element_type=jnp.float32
            )[0:64].astype(jnp.bfloat16)

    def gather_copy(half, group, kind, place):
        low = half * 4 + (2 if kind == 3 else 0)
        size = 2 if kind >= 2 else 4
        on_y = (half == 0) == (group is None)
        to = (at_y if on_y else at_z)(1 if kind % 2 == 0 else 3)
        block = kv.at[place[0], pl.ds(low, size), quarter(place[1])]
        index = 4 if group is None else group
        return pltpu.make_async_remote_copy(
            src_ref=block, dst_ref=block,
            send_sem=g_send.at[half, index, kind], recv_sem=g_recv.at[half, index, kind],
            device_id=to, device_id_type=MESH,
        )

    def launch(group, offset):
        for half in (0, 1):
            for kind in (0, 1):
                gather_copy(half, group, kind, chunk(half, offset, 0)).start()

    keep.wait()
    for copy in sent:
        copy.wait_recv()
    launch(None, 0)
    launch(0, 0)
    tables = []
    for d in range(1, 8):
        copy = pltpu.make_async_remote_copy(
            src_ref=table.at[s], dst_ref=table.at[s], send_sem=n_send.at[d], recv_sem=n_recv.at[d],
            device_id=at_s(d), device_id_type=MESH,
        )
        copy.start()
        tables.append(copy)
    each_far(lambda copy: copy.start())
    keep_w = pltpu.make_async_copy(
        w_down.at[:, pl.ds(pl.multiple_of(s * 896, 896), 896)],
        down_w.at[pl.ds(pl.multiple_of(s * 256, 256), 256)], w_sem.at[1],
    )
    keep_w.start()
    moved = []
    for d in range(1, 8):
        to = at_s(d)
        copy = pltpu.make_async_remote_copy(
            src_ref=w_down.at[:, pl.ds(pl.multiple_of(to[0] * 896, 896), 896)],
            dst_ref=down_w.at[pl.ds(pl.multiple_of(s * 256, 256), 256)],
            send_sem=d_send.at[d - 1], recv_sem=d_recv.at[d - 1],
            device_id=to, device_id_type=MESH,
        )
        copy.start()
        moved.append(copy)
    for kind in (0, 1):
        offset = 1 if kind == 0 else 3
        for half in (0, 1):
            gather_copy(half, None, kind, (y, z)).wait_recv()
            gather_copy(half, None, kind + 2, chunk(half, offset, 0)).start()
        launch(kind + 1, offset)
    for half in (0, 1):
        for kind in (2, 3):
            gather_copy(half, None, kind, (y, z)).wait_recv()
    launch(3, 2)
    for copy in tables:
        copy.wait_recv()
    build_weigh()
    attend(y, 1)

    def take_far(copy):
        if copy.is_remote:
            copy.wait_recv()
        else:
            copy.wait()

    each_far(take_far)
    attend(lax.rem(y + 2, 4), 1)

    def sides(i, _):
        for kind in (0, 1):
            for half in (0, 1):
                gather_copy(half, i, kind, (y, z)).wait_recv()
        attend(chunk(0, offset_of(i), 0)[0], 0)
        return 0

    lax.fori_loop(0, 4, sides, 0)

    def last(i, _):
        attend(lax.rem(y + 1 + 2 * i, 4), 1)
        return 0

    lax.fori_loop(0, 2, last, 0)

    for h in range(4):
        own = pl.ds(h * 128, 128)
        latent = (acc[own] / total[own, 0:1]).astype(jnp.bfloat16)
        head_out[:, h * 128:(h + 1) * 128] = jnp.dot(
            latent, w_uv[h], preferred_element_type=jnp.float32
        ).astype(jnp.bfloat16)
    get_w.wait()

    first = []
    for half in (0, 1):
        def project(t, _):
            lane = pl.multiple_of(t * 256, 256)
            both = []
            for k in (0, 1):
                column = pl.multiple_of(half * 3584 + k * 1792 + t * 256, 256)
                both.append(jnp.dot(
                    head_out[...], out_w[:, pl.ds(column, 256)], preferred_element_type=jnp.float32
                ).reshape(16, 8, 256))
            tile = jnp.concatenate(both, axis=1).astype(jnp.bfloat16)
            if half == 0:
                part[0, :, :, pl.ds(lane, 256)] = tile
            else:
                for p in range(16):
                    part[1, (p % 4) * 4 + p // 4, :, pl.ds(lane, 256)] = tile[p]
            return 0

        lax.fori_loop(0, 7, project, 0)
        for d in (1, 2, 3):
            to, line = (at_y(d), lax.rem(y + d, 4)) if half == 0 else (at_z(d), lax.rem(z + d, 4))
            copy = pltpu.make_async_remote_copy(
                src_ref=part.at[half, pl.ds(line * 4, 4)], dst_ref=part_in.at[half, d - 1],
                send_sem=r_send.at[half, 0, d - 1], recv_sem=r_recv.at[half, 0, d - 1],
                device_id=to, device_id_type=MESH,
            )
            copy.start()
            first.append(copy)
    second = []
    for half in (0, 1):
        for d in (1, 2, 3):
            first[half * 3 + d - 1].wait_recv()
        own = y if half == 0 else z

        def add(k, _):
            value = part[half, own * 4 + k].astype(jnp.float32)
            for d in range(3):
                value = value + part_in[half, d, k].astype(jnp.float32)
            summed[half, k] = value.astype(jnp.bfloat16)
            return 0

        lax.fori_loop(0, 4, add, 0)
        for d in (1, 2, 3):
            to, line = (at_z(d), lax.rem(z + d, 4)) if half == 0 else (at_y(d), lax.rem(y + d, 4))
            copy = pltpu.make_async_remote_copy(
                src_ref=summed.at[half, line], dst_ref=summed_in.at[half, d - 1],
                send_sem=r_send.at[half, 1, d - 1], recv_sem=r_recv.at[half, 1, d - 1],
                device_id=to, device_id_type=MESH,
            )
            copy.start()
            second.append(copy)
    squares = jnp.zeros((8, 1), jnp.float32)
    for half in (0, 1):
        for d in (1, 2, 3):
            second[half * 3 + d - 1].wait_recv()
        value = summed[half, z if half == 0 else y].astype(jnp.float32)
        for d in range(3):
            value = value + summed_in[half, d].astype(jnp.float32)
        for k in (0, 1):
            q = 2 * half + k
            row = residual[:, q * 1792:(q + 1) * 1792].astype(jnp.float32) + value[k * 8:(k + 1) * 8]
            rows[q] = row
            squares = squares + jnp.sum(row * row, axis=1, keepdims=True)
    norm = lax.rsqrt(squares / 7168.0 + 1e-06)
    for q in (0, 2):
        two = jnp.concatenate([rows[q] * norm, rows[q + 1] * norm], axis=0)
        normed[0, q * 8:(q + 2) * 8] = two.astype(jnp.bfloat16)

    swap = copy_to(normed.at[0], normed.at[1], n_send.at[0], n_recv.at[0], at_s(4))
    swap.start()

    def dispatch(side, k, dz):
        to = on_ep(offset_of(k) + dz, dz)
        return copy_to(
            outgoing.at[side, to], arrived.at[side, e], t_send.at[side, k, dz], t_recv.at[side, k, dz], (s, to)
        )

    def give_back(k, dz):
        to = on_ep(4 - offset_of(k) + dz, dz)
        return copy_to(y_part.at[k, lax.rem(z + dz, 4)], returned.at[e], b_send.at[k, dz], b_recv.at[k, dz], (s, to))

    def gather(k, kind):
        to = at_s((2, 6)[kind]) if kind < 2 else (sibling, e)
        block = lax.rem(s + (0, 0, 0, 4, 6, 2)[kind], 8)
        ref = x_rows.at[k, pl.ds(pl.multiple_of(block * 16, 16), 16)]
        return copy_to(ref, ref, a_send.at[k, kind], a_recv.at[k, kind], to)

    def share(k, kind):
        to = at_s((2, 6, 4)[kind]) if kind < 3 else (sibling, e)
        block = lax.rem(s + (0, 0, 0, 0, 6, 2, 4)[kind], 8)
        ref = hid.at[k, :, pl.ds(pl.multiple_of(block * 256, 256), 256)]
        return copy_to(ref, ref, h_send.at[k, kind], h_recv.at[k, kind], to)

    def spread_rows(side):
        group = lax.rem(s + 4 * side, 8)
        to_row = lax.broadcasted_iota(jnp.int32, (256, 64), 0)
        from_pair = lax.broadcasted_iota(jnp.int32, (256, 64), 1)
        widen = (from_pair == (to_row // 16) * 4 + to_row % 4).astype(jnp.bfloat16)
        held = jnp.dot(
            widen, (table[group] > 0).astype(jnp.bfloat16), preferred_element_type=jnp.float32
        )[:, 0:32]
        row_quarter = lax.broadcasted_iota(jnp.int32, (256, 32), 0) // 4 % 4
        col_quarter = lax.broadcasted_iota(jnp.int32, (256, 32), 1) // 8
        place = jnp.where(row_quarter == col_quarter, held, 0.0).astype(jnp.bfloat16)
        outgoing[side] = jnp.dot(
            place, normed[side], preferred_element_type=jnp.float32
        ).astype(jnp.bfloat16).reshape(16, 16, 1792)
        arrived[side, e] = outgoing[side, e]

    def send_rows(side, k, own=False):
        for dz in (2, 1, 3) if own else (2, 1, 3, 0):
            dispatch(side, k, dz).start()

    spread_rows(0)
    send_rows(0, 0, True)
    send_rows(0, 1)
    swap.wait_recv()
    spread_rows(1)
    send_rows(1, 0, True)

    rows16 = lax.broadcasted_iota(jnp.int32, (16, 64), 0)
    cols64 = lax.broadcasted_iota(jnp.int32, (16, 64), 1)

    def enter(side, k):
        for dz in range(1, 4):
            dispatch(side, k, dz).wait_recv()

        @pl.when(k > 0)
        def _():
            dispatch(side, k, 0).wait_recv()

        block = jnp.concatenate([
            arrived[side, lax.rem(y - z + 8 - offset_of(k) + i, 4) * 4 + i] for i in range(4)
        ], axis=0)
        low = pl.multiple_of(lax.rem(s + 4 * side, 8) * 16, 16)
        for q in range(4):
            take = (cols64 == (rows16 // 4) * 16 + q * 4 + rows16 % 4).astype(jnp.bfloat16)
            x_rows[k, pl.ds(low, 16), q * 1792:(q + 1) * 1792] = jnp.dot(
                take, block, preferred_element_type=jnp.float32
            ).astype(jnp.bfloat16)
        for kind in ((0, 1, 2), (3,))[side]:
            gather(k, kind).start()

    def pass_on(k):
        for kind in (0, 1):
            gather(k, kind).wait_recv()
            gather(k, kind + 4).start()

    def hidden(k):
        for kind in range(2, 6):
            gather(k, kind).wait_recv()
        pre[...] = jnp.zeros_like(pre)

        def add(q, _):
            low = pl.multiple_of(q * 1792, 1792)
            pre[...] += jnp.dot(
                x_rows[k, :, pl.ds(low, 1792)], in_w[pl.ds(low, 1792)], preferred_element_type=jnp.float32
            )
            return 0

        lax.fori_loop(0, 4, add, 0)
        gate = pre[:, 0:256]
        hid[k, :, pl.ds(pl.multiple_of(s * 256, 256), 256)] = (
            gate / (1.0 + jnp.exp(-gate)) * pre[:, 256:512]
        ).astype(jnp.bfloat16)
        for kind in range(4):
            share(k, kind).start()

    to128 = lax.broadcasted_iota(jnp.int32, (128, 128), 0)
    from128 = lax.broadcasted_iota(jnp.int32, (128, 128), 1)

    def project(k):
        for kind in range(3):
            share(k, kind).wait_recv()
            share(k, kind + 4).start()
        for kind in range(3, 7):
            share(k, kind).wait_recv()
        value = jnp.dot(hid[k], down_w[...], preferred_element_type=jnp.float32).astype(jnp.bfloat16)
        order = (from128 == (to128 // 4 % 8) * 16 + (to128 // 32) * 4 + to128 % 4).astype(jnp.bfloat16)
        y_part[k] = jnp.dot(order, value, preferred_element_type=jnp.float32).astype(jnp.bfloat16).reshape(4, 32, 896)
        for dz in range(1, 4):
            give_back(k, dz).start()

        @pl.when(k > 0)
        def _():
            give_back(k, 0).start()

        @pl.when(k == 0)
        def _():
            returned[e] = y_part[k, z]

    def step(t, _):
        @pl.when(t < 4)
        def _():
            enter(0, t)

        @pl.when(t < 2)
        def _():
            send_rows(0, t + 2)

        @pl.when(t < 3)
        def _():
            send_rows(1, t + 1)

        @pl.when(t == 1)
        def _():
            for load in get_in:
                load.wait()

        @pl.when((t >= 1) & (t < 5))
        def _():
            enter(1, t - 1)
            pass_on(t - 1)
            hidden(t - 1)

        @pl.when(t == 2)
        def _():
            keep_w.wait()
            for copy in moved:
                copy.wait_recv()

        @pl.when(t >= 2)
        def _():
            project(t - 2)

        return 0

    lax.fori_loop(0, 6, step, 0)

    for k in range(4):
        for dz in range(4):
            if k or dz:
                give_back(k, dz).wait_recv()
    back = returned[...].reshape(512, 896)
    mix_out[...] = jnp.dot(weigh[0], back, preferred_element_type=jnp.float32) + jnp.dot(
        weigh[1], back, preferred_element_type=jnp.float32
    )
    columns = pl.ds(pl.multiple_of(s * 896, 896), 896)
    handed = []
    for d in (4, 2, 6, 3, 5, 1, 7):
        to = at_s(d)
        copy = copy_to(
            mix_out.at[pl.ds(pl.multiple_of(to[0] * 8, 8), 8)], mix_in.at[:, columns],
            m_send.at[d - 1], m_recv.at[d - 1], to,
        )
        copy.start()
        handed.append(copy)
    mix_in[:, columns] = mix_out[pl.ds(pl.multiple_of(s * 8, 8), 8)]
    for copy in handed:
        copy.wait_recv()
    for q in range(4):
        own = slice(q * 1792, (q + 1) * 1792)
        out[:, own] = (rows[q] + mix_in[:, own]).astype(jnp.bfloat16)

    for copy in handed + tables + [swap] + moved:
        copy.wait_send()
    for k in range(4):
        for dz in range(4):
            if k or dz:
                dispatch(0, k, dz).wait_send()
                dispatch(1, k, dz).wait_send()
                give_back(k, dz).wait_send()
        for kind in range(6):
            gather(k, kind).wait_send()
        for kind in range(7):
            share(k, kind).wait_send()
    for copy in sent + first + second:
        copy.wait_send()
    each_far(lambda copy: copy.wait_send() if copy.is_remote else None)
    for half in (0, 1):
        for group in range(5):
            for kind in range(4 if group == 4 else 2):
                gather_copy(half, group if group < 4 else None, kind, (y, z)).wait_send()


def layer_call(*arrays):
    vmem = pl.BlockSpec(memory_space=pltpu.VMEM)
    anywhere = pl.BlockSpec(memory_space=pl.ANY)
    bf16, f32 = jnp.bfloat16, jnp.float32
    dma = pltpu.SemaphoreType.DMA
    return pl.pallas_call(
        layer_kernel,
        name="layer",
        out_shape=jax.ShapeDtypeStruct((8, 7168), bf16),
        in_specs=[anywhere, anywhere, vmem, vmem, vmem, anywhere, vmem, vmem, vmem, anywhere, anywhere, anywhere],
        out_specs=vmem,
        scratch_shapes=[
            pltpu.VMEM((4, 8, 576, 128), bf16),
            pltpu.VMEM((512, 576), bf16),
            pltpu.VMEM((4, 2, 128, 512), f32),
            pltpu.VMEM((512, 128), f32),
            pltpu.VMEM((512, 128), f32),
            pltpu.VMEM((512, 512), f32),
            pltpu.VMEM((128, 512), bf16),
            pltpu.VMEM((512, 7168), bf16),
            pltpu.VMEM((2, 16, 16, 1792), bf16),
            pltpu.VMEM((2, 3, 4, 16, 1792), bf16),
            pltpu.VMEM((2, 4, 16, 1792), bf16),
            pltpu.VMEM((2, 3, 16, 1792), bf16),
            pltpu.VMEM((4, 8, 1792), f32),
            pltpu.VMEM((8, 64, 128), f32),
            pltpu.VMEM((2, 64, 512), bf16),
            pltpu.VMEM((2, 32, 1792), bf16),
            pltpu.VMEM((2, 16, 16, 1792), bf16),
            pltpu.VMEM((2, 16, 16, 1792), bf16),
            pltpu.VMEM((4, 128, 7168), bf16),
            pltpu.VMEM((7168, 512), bf16),
            pltpu.VMEM((2048, 896), bf16),
            pltpu.VMEM((128, 512), f32),
            pltpu.VMEM((4, 128, 2048), bf16),
            pltpu.VMEM((4, 4, 32, 896), bf16),
            pltpu.VMEM((16, 32, 896), bf16),
            pltpu.VMEM((64, 896), f32),
            pltpu.VMEM((8, 7168), f32),
            dma((2, 7)), dma((2, 7)),
            dma((2, 5, 4)), dma((2, 5, 4)),
            dma((2, 2, 3)), dma((2, 2, 3)),
            dma((7,)), dma((7,)),
            dma((6,)),
            dma((8,)), dma((8,)),
            dma((2, 4, 4)), dma((2, 4, 4)),
            dma((4, 6)), dma((4, 6)),
            dma((4, 7)), dma((4, 7)),
            dma((4, 4)), dma((4, 4)),
            dma((7,)), dma((7,)),
        ],
        compiler_params=pltpu.CompilerParams(
            collective_id=0, has_side_effects=True, vmem_limit_bytes=60 << 20
        ),
    )(*arrays)


def serve_kernel(group_passages, passage_place, latents, served, served_far, sem):
    s, e = lax.axis_index("store"), lax.axis_index("ep")
    y, z = e // 4, e % 4
    copies = []
    for g in range(8):
        def piece(j, q, dst, i):
            place = passage_place[group_passages[g * 32 + s * 4 + j]] - s * 32
            copy = pltpu.make_async_copy(
                latents.at[place, pl.ds(pl.multiple_of(q * 144, 16), 144)], dst, sem.at[g, i]
            )
            copy.start()
            copies.append(copy)

        piece(y, z, served.at[g], 4)
        for i in range(4):
            piece(
                jnp.where(s < 4, i, lax.rem(y + 2, 4)), jnp.where(s < 4, lax.rem(z + 2, 4), i),
                served_far.at[g, i], i,
            )
    for copy in copies:
        copy.wait()


def serve(latent_store, group_passages, passage_place):
    smem = pl.BlockSpec(memory_space=pltpu.SMEM)
    vmem = pl.BlockSpec(memory_space=pltpu.VMEM)
    anywhere = pl.BlockSpec(memory_space=pl.ANY)
    return pl.pallas_call(
        serve_kernel,
        name="serve",
        out_shape=(
            jax.ShapeDtypeStruct((8, 144, 128), jnp.bfloat16),
            jax.ShapeDtypeStruct((8, 4, 144, 128), jnp.bfloat16),
        ),
        in_specs=[smem, smem, anywhere],
        out_specs=(vmem, vmem),
        scratch_shapes=[pltpu.SemaphoreType.DMA((8, 5))],
    )(group_passages, passage_place, jnp.swapaxes(latent_store, 1, 2))


def body(
    queries, residual_in, latent_store, group_passages, row_slots, passage_place, w_uv, w_out,
    expert_ids, expert_gates, w_gate, w_up, w_down,
):
    served, served_far = serve(latent_store, group_passages, passage_place)
    return layer_call(
        served, served_far, queries, row_slots.T, w_uv, w_out, residual_in,
        expert_ids.T, expert_gates.T, w_gate[0], w_up[0], w_down[0],
    )


def solution(mesh):
    return jax.shard_map(
        body,
        mesh=mesh,
        in_specs=(
            P("store", "ep"),
            P(("store", "ep"), None),
            P("store", None, None),
            P(),
            P("store", None),
            P(),
            P("ep", None, None),
            P("ep", None),
            P(("store", "ep"), None),
            P(("store", "ep"), None),
            P("ep", None, "store"),
            P("ep", None, "store"),
            P("ep", "store", None),
        ),
        out_specs=P(("store", "ep"), None),
        check_vma=False,
    )
```

```python
import functools

import jax
import jax.numpy as jnp
from jax import lax
from jax.experimental import pallas as pl
from jax.experimental.pallas import tpu as pltpu
from jax.sharding import PartitionSpec as P

SCALE = 192.0 ** (-0.5) * 1.4426950408889634
MESH = pl.DeviceIdType.MESH
LOW = -1e29
FAR_LOW = 1e30


def offset_of(i):
    return i + i // 2 - 2 * (i // 3)


def layer_kernel(
    served, served_far, queries, row_slots, w_uv, w_out, residual, ids, gates, w_gate, w_up, w_down,
    out,
    kv, heads, mask, top, total, acc, head_out, out_w, part, part_in, summed, summed_in, rows,
    table, weigh, places, normed, outgoing, arrived, x_rows, in_w, down_w, pre, hid, y_part, returned, mix_out, mix_in,
    x_send, x_recv, g_send, g_recv, r_send, r_recv, d_send, d_recv, w_sem,
    n_send, n_recv, t_send, t_recv, a_send, a_recv, h_send, h_recv, b_send, b_recv, m_send, m_recv,
):
    s = lax.axis_index("store")
    e = lax.axis_index("ep")
    y, z = e // 4, e % 4

    def at_y(d):
        return (s, lax.rem(y + d, 4) * 4 + z)

    def at_z(d):
        return (s, y * 4 + lax.rem(z + d, 4))

    def at_s(d):
        return (lax.rem(s + d, 8), e)

    def quarter(q):
        return pl.ds(pl.multiple_of(q * 144, 16), 144)

    sibling = s + 1 - 2 * (s % 2)

    def on_ep(dy, dz):
        return lax.rem(y + dy, 4) * 4 + lax.rem(z + dz, 4)

    peers = [at_s(d) for d in range(1, 8)]
    peers += [(s, on_ep(dy, dz)) for dy in range(4) for dz in range(4) if dy or dz]
    barrier = pltpu.get_barrier_semaphore()
    for peer in peers:
        pl.semaphore_signal(barrier, inc=1, device_id=peer, device_id_type=MESH)
    get_w = pltpu.make_async_copy(w_out, out_w, w_sem.at[0])
    get_in = [
        pltpu.make_async_copy(w_gate, in_w.at[:, 0:256], w_sem.at[4]),
        pltpu.make_async_copy(w_up, in_w.at[:, 256:512], w_sem.at[5]),
    ]
    for load in [get_w] + get_in:
        load.start()

    lane_row = lax.broadcasted_iota(jnp.int32, (1, 128), 1) % 8
    repeat = (lax.broadcasted_iota(jnp.int32, (8, 1), 0) == lane_row).astype(jnp.float32)
    wide_ids = jnp.dot(ids[...].astype(jnp.float32), repeat, preferred_element_type=jnp.float32)
    wide_gates = jnp.dot(
        gates[...], repeat, preferred_element_type=jnp.float32, precision=lax.Precision.HIGHEST
    )
    pair = lax.broadcasted_iota(jnp.int32, (64, 1), 0)
    expert = (pair // 4).astype(jnp.float32)
    routed = jnp.zeros((64, 128), jnp.float32)
    gate = jnp.zeros((64, 128), jnp.float32)
    for i in range(4):
        named = (wide_ids[i:i + 1] == expert).astype(jnp.float32)
        routed = routed + named
        gate = gate + named * wide_gates[i:i + 1]
    before = lax.broadcasted_iota(jnp.int32, (128, 1), 0)
    upto = lax.broadcasted_iota(jnp.int32, (1, 128), 1) % 8
    earlier = jnp.dot(
        routed.astype(jnp.bfloat16), (before < upto).astype(jnp.bfloat16), preferred_element_type=jnp.float32
    )
    table[s] = jnp.where((routed > 0.5) & (earlier == (pair % 4).astype(jnp.float32)), gate, 0.0)
    pl.semaphore_wait(barrier, len(peers))

    sent = []
    for d in range(1, 8):
        to = at_s(d)
        copy = pltpu.make_async_remote_copy(
            src_ref=served.at[to[0]], dst_ref=kv.at[y, s, quarter(z)],
            send_sem=x_send.at[0, d - 1], recv_sem=x_recv.at[0, d - 1],
            device_id=to, device_id_type=MESH,
        )
        copy.start()
        sent.append(copy)
    keep = pltpu.make_async_copy(served.at[s], kv.at[y, s, quarter(z)], w_sem.at[2])
    keep.start()

    def copy_to(src, dst, send, recv, device):
        return pltpu.make_async_remote_copy(
            src_ref=src, dst_ref=dst, send_sem=send, recv_sem=recv, device_id=device, device_id_type=MESH
        )

    def far_copies(whole):
        def target(ref):
            return ref.at[lax.rem(y + 2, 4), s] if whole else ref.at[:, s, quarter(lax.rem(z + 2, 4))]

        def source(g):
            return served_far.at[g].reshape(576, 128) if whole else served_far.at[g]

        return [
            pltpu.make_async_remote_copy(
                src_ref=source(at_s(d)[0]), dst_ref=target(kv),
                send_sem=x_send.at[1, d - 1], recv_sem=x_recv.at[1, d - 1],
                device_id=at_s(d), device_id_type=MESH,
            )
            for d in range(1, 8)
        ] + [pltpu.make_async_copy(source(s), target(kv), w_sem.at[3])]

    def each_far(act):
        for whole in (False, True):
            @pl.when((s >= 4) if whole else (s < 4))
            def _():
                for copy in far_copies(whole):
                    act(copy)

    tables = []
    for d in range(1, 8):
        copy = pltpu.make_async_remote_copy(
            src_ref=table.at[s], dst_ref=table.at[s], send_sem=n_send.at[d], recv_sem=n_recv.at[d],
            device_id=at_s(d), device_id_type=MESH,
        )
        copy.start()
        tables.append(copy)
    each_far(lambda copy: copy.start())

    for h in range(4):
        heads[h * 128:(h + 1) * 128] = queries[:, h * 576:(h + 1) * 576]
    slot = lax.broadcasted_iota(jnp.int32, (32, 1), 0)
    chosen = jnp.zeros((32, 128), jnp.bool_)
    for i in range(16):
        chosen = chosen | (row_slots[i:i + 1] == slot)
    chosen = chosen.astype(jnp.bfloat16)
    slot_row = lax.broadcasted_iota(jnp.int32, (32, 1), 0)
    token_col = lax.broadcasted_iota(jnp.int32, (1, 512), 1)
    for j in range(4):
        for half in (0, 1):
            spread = (slot_row == (token_col // 128 + 4 * half) * 4 + j).astype(jnp.bfloat16)
            live = lax.dot_general(
                chosen, spread, (((0,), (0,)), ((), ())), preferred_element_type=jnp.float32
            )
            mask[j, half] = (live - 1.0) * FAR_LOW
    top[...] = jnp.full_like(top, LOW)
    total[...] = jnp.zeros_like(total)
    acc[...] = jnp.zeros_like(acc)

    def chunk(half, first, second):
        dy, dz = (first, second) if half == 0 else (second, first)
        return lax.rem(y - dy + 4, 4), lax.rem(z - dz + 4, 4)

    def attend(j, half):
        keys = jnp.concatenate([kv[j, half * 4 + i] for i in range(4)], axis=1)
        scores = jnp.dot(heads[...], keys, preferred_element_type=jnp.float32) * SCALE
        scores = (scores.reshape(4, 128, 512) + mask[j, half]).reshape(512, 512)
        old = top[...]
        new = jnp.maximum(old, jnp.max(scores, axis=1, keepdims=True))
        exponent = jnp.exp2(scores - new[:, 0:1])
        scale = jnp.exp2(old - new)
        top[...] = new
        total[...] = total[...] * scale + jnp.sum(exponent, axis=1, keepdims=True)
        acc[...] = acc[...] * scale[:, 0:1] + lax.dot_general(
            exponent.astype(jnp.bfloat16), keys[0:512], (((1,), (1,)), ((), ())),
            preferred_element_type=jnp.float32,
        )

    def build_weigh():
        lane = lax.broadcasted_iota(jnp.int32, (1, 128), 1)
        gated = jnp.concatenate([jnp.where(lane // 8 == g, table[g], 0.0) for g in range(8)], axis=0)
        from_row = lax.broadcasted_iota(jnp.int32, (512, 1), 0)
        to_col = lax.broadcasted_iota(jnp.int32, (1, 512), 1)
        place = (to_col // 4 % 8) * 64 + (to_col // 32) * 4 + to_col % 4
        move = (from_row == place).astype(jnp.bfloat16)
        high = gated.astype(jnp.bfloat16)
        low = (gated - high.astype(jnp.float32)).astype(jnp.bfloat16)
        for i, held in ((0, high), (1, low)):
            weigh[i] = lax.dot_general(
                held, move, (((0,), (0,)), ((), ())), preferred_element_type=jnp.float32
            )[0:64].astype(jnp.bfloat16)

    def build_place(side):
        group = lax.rem(s + 4 * side, 8)
        to_row = lax.broadcasted_iota(jnp.int32, (256, 1), 0)
        from_pair = lax.broadcasted_iota(jnp.int32, (1, 64), 1)
        widen = (from_pair == (to_row // 16) * 4 + to_row % 4).astype(jnp.bfloat16)
        held = jnp.dot(
            widen, (table[group] > 0).astype(jnp.bfloat16), preferred_element_type=jnp.float32
        )[:, 0:32]
        row_quarter = lax.broadcasted_iota(jnp.int32, (256, 1), 0) // 4 % 4
        col_quarter = lax.broadcasted_iota(jnp.int32, (1, 32), 1) // 8
        places[side] = jnp.where(row_quarter == col_quarter, held, 0.0).astype(jnp.bfloat16)
    def gather_copy(half, group, kind, place):
        low = half * 4 + (2 if kind == 3 else 0)
        size = 2 if kind >= 2 else 4
        on_y = (half == 0) == (group is None)
        to = (at_y if on_y else at_z)(1 if kind % 2 == 0 else 3)
        block = kv.at[place[0], pl.ds(low, size), quarter(place[1])]
        index = 4 if group is None else group
        return pltpu.make_async_remote_copy(
            src_ref=block, dst_ref=block,
            send_sem=g_send.at[half, index, kind], recv_sem=g_recv.at[half, index, kind],
            device_id=to, device_id_type=MESH,
        )

    def launch(group, offset):
        for half in (0, 1):
            for kind in (0, 1):
                gather_copy(half, group, kind, chunk(half, offset, 0)).start()

    keep.wait()
    for copy in sent:
        copy.wait_recv()
    launch(None, 0)
    launch(0, 0)
    keep_w = pltpu.make_async_copy(
        w_down.at[:, pl.ds(pl.multiple_of(s * 896, 896), 896)],
        down_w.at[pl.ds(pl.multiple_of(s * 256, 256), 256)], w_sem.at[1],
    )
    keep_w.start()
    moved = []
    for d in range(1, 8):
        to = at_s(d)
        copy = pltpu.make_async_remote_copy(
            src_ref=w_down.at[:, pl.ds(pl.multiple_of(to[0] * 896, 896), 896)],
            dst_ref=down_w.at[pl.ds(pl.multiple_of(s * 256, 256), 256)],
            send_sem=d_send.at[d - 1], recv_sem=d_recv.at[d - 1],
            device_id=to, device_id_type=MESH,
        )
        if d != 4:
            copy.start()
        moved.append(copy)
    for kind in (0, 1):
        offset = 1 if kind == 0 else 3
        for half in (0, 1):
            gather_copy(half, None, kind, (y, z)).wait_recv()
            gather_copy(half, None, kind + 2, chunk(half, offset, 0)).start()
    launch(1, 1)
    launch(2, 3)
    for half in (0, 1):
        for kind in (2, 3):
            gather_copy(half, None, kind, (y, z)).wait_recv()
    launch(3, 2)
    attend(y, 1)

    def take_far(copy):
        if copy.is_remote:
            copy.wait_recv()
        else:
            copy.wait()

    each_far(take_far)
    attend(lax.rem(y + 2, 4), 1)

    def sides(i, _):
        for kind in (0, 1):
            for half in (0, 1):
                gather_copy(half, i, kind, (y, z)).wait_recv()
        attend(chunk(0, offset_of(i), 0)[0], 0)
        return 0

    lax.fori_loop(0, 4, sides, 0)

    def last(i, _):
        attend(lax.rem(y + 1 + 2 * i, 4), 1)
        return 0

    lax.fori_loop(0, 2, last, 0)

    for h in range(4):
        own = pl.ds(h * 128, 128)
        latent = (acc[own] / total[own, 0:1]).astype(jnp.bfloat16)
        head_out[:, h * 128:(h + 1) * 128] = jnp.dot(
            latent, w_uv[h], preferred_element_type=jnp.float32
        ).astype(jnp.bfloat16)
    get_w.wait()

    first = []
    for half in (0, 1):
        def project(t, _):
            lane = pl.multiple_of(t * 256, 256)
            both = []
            for k in (0, 1):
                column = pl.multiple_of(half * 3584 + k * 1792 + t * 256, 256)
                both.append(jnp.dot(
                    head_out[...], out_w[:, pl.ds(column, 256)], preferred_element_type=jnp.float32
                ).reshape(16, 8, 256))
            tile = jnp.concatenate(both, axis=1).astype(jnp.bfloat16)
            if half == 0:
                part[0, :, :, pl.ds(lane, 256)] = tile
            else:
                for p in range(16):
                    part[1, (p % 4) * 4 + p // 4, :, pl.ds(lane, 256)] = tile[p]
            return 0

        lax.fori_loop(0, 7, project, 0)
        for d in (1, 2, 3):
            to, line = (at_y(d), lax.rem(y + d, 4)) if half == 0 else (at_z(d), lax.rem(z + d, 4))
            copy = pltpu.make_async_remote_copy(
                src_ref=part.at[half, pl.ds(line * 4, 4)], dst_ref=part_in.at[half, d - 1],
                send_sem=r_send.at[half, 0, d - 1], recv_sem=r_recv.at[half, 0, d - 1],
                device_id=to, device_id_type=MESH,
            )
            copy.start()
            first.append(copy)
    for copy in tables:
        copy.wait_recv()
    build_place(0)
    build_place(1)
    second = []
    for half in (0, 1):
        for d in (1, 2, 3):
            first[half * 3 + d - 1].wait_recv()
        own = y if half == 0 else z

        def add(k, _):
            value = part[half, own * 4 + k].astype(jnp.float32)
            for d in range(3):
                value = value + part_in[half, d, k].astype(jnp.float32)
            summed[half, k] = value.astype(jnp.bfloat16)
            return 0

        lax.fori_loop(0, 4, add, 0)
        for d in (1, 2, 3):
            to, line = (at_z(d), lax.rem(z + d, 4)) if half == 0 else (at_y(d), lax.rem(y + d, 4))
            copy = pltpu.make_async_remote_copy(
                src_ref=summed.at[half, line], dst_ref=summed_in.at[half, d - 1],
                send_sem=r_send.at[half, 1, d - 1], recv_sem=r_recv.at[half, 1, d - 1],
                device_id=to, device_id_type=MESH,
            )
            copy.start()
            second.append(copy)
    squares = jnp.zeros((8, 1), jnp.float32)
    for half in (0, 1):
        for d in (1, 2, 3):
            second[half * 3 + d - 1].wait_recv()
        value = summed[half, z if half == 0 else y].astype(jnp.float32)
        for d in range(3):
            value = value + summed_in[half, d].astype(jnp.float32)
        for k in (0, 1):
            q = 2 * half + k
            row = residual[:, q * 1792:(q + 1) * 1792].astype(jnp.float32) + value[k * 8:(k + 1) * 8]
            rows[q] = row
            squares = squares + jnp.sum(row * row, axis=1, keepdims=True)
    norm = lax.rsqrt(squares / 7168.0 + 1e-06)
    for q in (0, 2):
        two = jnp.concatenate([rows[q] * norm, rows[q + 1] * norm], axis=0)
        normed[0, q * 8:(q + 2) * 8] = two.astype(jnp.bfloat16)

    swap = copy_to(normed.at[0], normed.at[1], n_send.at[0], n_recv.at[0], at_s(4))
    swap.start()
    moved[3].start()

    def dispatch(side, k, dz):
        to = on_ep(offset_of(k) + dz, dz)
        return copy_to(
            outgoing.at[side, to], arrived.at[side, e], t_send.at[side, k, dz], t_recv.at[side, k, dz], (s, to)
        )

    def give_back(k, dz):
        to = on_ep(4 - offset_of(k) + dz, dz)
        return copy_to(y_part.at[k, lax.rem(z + dz, 4)], returned.at[e], b_send.at[k, dz], b_recv.at[k, dz], (s, to))

    def gather(k, kind):
        to = at_s((2, 6)[kind]) if kind < 2 else (sibling, e)
        block = lax.rem(s + (0, 0, 0, 4, 6, 2)[kind], 8)
        ref = x_rows.at[k, pl.ds(pl.multiple_of(block * 16, 16), 16)]
        return copy_to(ref, ref, a_send.at[k, kind], a_recv.at[k, kind], to)

    def share(k, kind):
        to = at_s((2, 6, 4)[kind]) if kind < 3 else (sibling, e)
        block = lax.rem(s + (0, 0, 0, 0, 6, 2, 4)[kind], 8)
        ref = hid.at[k, :, pl.ds(pl.multiple_of(block * 256, 256), 256)]
        return copy_to(ref, ref, h_send.at[k, kind], h_recv.at[k, kind], to)

    def spread_rows(side):
        outgoing[side] = jnp.dot(
            places[side], normed[side], preferred_element_type=jnp.float32
        ).astype(jnp.bfloat16).reshape(16, 16, 1792)
        arrived[side, e] = outgoing[side, e]

    def send_rows(side, k, own=False):
        for dz in (2, 1, 3) if own else (2, 1, 3, 0):
            dispatch(side, k, dz).start()

    spread_rows(0)
    send_rows(0, 0, True)
    send_rows(0, 1)
    swap.wait_recv()
    spread_rows(1)
    send_rows(1, 0, True)

    rows16 = lax.broadcasted_iota(jnp.int32, (16, 1), 0)
    cols64 = lax.broadcasted_iota(jnp.int32, (1, 64), 1)

    def enter(side, k):
        for dz in range(1, 4):
            dispatch(side, k, dz).wait_recv()

        @pl.when(k > 0)
        def _():
            dispatch(side, k, 0).wait_recv()

        block = jnp.concatenate([
            arrived[side, lax.rem(y - z + 8 - offset_of(k) + i, 4) * 4 + i] for i in range(4)
        ], axis=0)
        low = pl.multiple_of(lax.rem(s + 4 * side, 8) * 16, 16)
        for q in range(4):
            take = (cols64 == (rows16 // 4) * 16 + q * 4 + rows16 % 4).astype(jnp.bfloat16)
            x_rows[k, pl.ds(low, 16), q * 1792:(q + 1) * 1792] = jnp.dot(
                take, block, preferred_element_type=jnp.float32
            ).astype(jnp.bfloat16)
        for kind in ((0, 1, 2), (3,))[side]:
            gather(k, kind).start()

    def pass_on(k):
        for kind in (0, 1):
            gather(k, kind).wait_recv()
            gather(k, kind + 4).start()

    def hidden(k):
        for kind in range(2, 6):
            gather(k, kind).wait_recv()
        pre[...] = jnp.zeros_like(pre)

        def add(q, _):
            low = pl.multiple_of(q * 1792, 1792)
            pre[...] += jnp.dot(
                x_rows[k, :, pl.ds(low, 1792)], in_w[pl.ds(low, 1792)], preferred_element_type=jnp.float32
            )
            return 0

        lax.fori_loop(0, 4, add, 0)
        gate = pre[:, 0:256]
        hid[k, :, pl.ds(pl.multiple_of(s * 256, 256), 256)] = (
            gate / (1.0 + jnp.exp(-gate)) * pre[:, 256:512]
        ).astype(jnp.bfloat16)
        for kind in range(4):
            share(k, kind).start()

    to128 = lax.broadcasted_iota(jnp.int32, (128, 1), 0)
    from128 = lax.broadcasted_iota(jnp.int32, (1, 128), 1)

    def project(k):
        for kind in range(3):
            share(k, kind).wait_recv()
            share(k, kind + 4).start()
        for kind in range(3, 7):
            share(k, kind).wait_recv()
        value = jnp.dot(hid[k], down_w[...], preferred_element_type=jnp.float32).astype(jnp.bfloat16)
        order = (from128 == (to128 // 4 % 8) * 16 + (to128 // 32) * 4 + to128 % 4).astype(jnp.bfloat16)
        y_part[k] = jnp.dot(order, value, preferred_element_type=jnp.float32).astype(jnp.bfloat16).reshape(4, 32, 896)
        for dz in range(1, 4):
            give_back(k, dz).start()

        @pl.when(k > 0)
        def _():
            give_back(k, 0).start()

        @pl.when(k == 0)
        def _():
            returned[e] = y_part[k, z]

    def step(t, _):
        @pl.when(t < 4)
        def _():
            enter(0, t)

        @pl.when(t < 2)
        def _():
            send_rows(0, t + 2)

        @pl.when(t < 3)
        def _():
            send_rows(1, t + 1)

        @pl.when(t == 0)
        def _():
            build_weigh()

        @pl.when(t == 1)
        def _():
            for load in get_in:
                load.wait()

        @pl.when((t >= 1) & (t < 5))
        def _():
            enter(1, t - 1)
            pass_on(t - 1)
            hidden(t - 1)

        @pl.when(t == 2)
        def _():
            keep_w.wait()
            for copy in moved:
                copy.wait_recv()

        @pl.when(t >= 2)
        def _():
            project(t - 2)

        return 0

    lax.fori_loop(0, 6, step, 0)

    for k in range(4):
        for dz in range(4):
            if k or dz:
                give_back(k, dz).wait_recv()
    back = returned[...].reshape(512, 896)
    mix_out[...] = jnp.dot(weigh[0], back, preferred_element_type=jnp.float32) + jnp.dot(
        weigh[1], back, preferred_element_type=jnp.float32
    )
    columns = pl.ds(pl.multiple_of(s * 896, 896), 896)
    handed = []
    for d in (4, 2, 6, 3, 5, 1, 7):
        to = at_s(d)
        copy = copy_to(
            mix_out.at[pl.ds(pl.multiple_of(to[0] * 8, 8), 8)], mix_in.at[:, columns],
            m_send.at[d - 1], m_recv.at[d - 1], to,
        )
        copy.start()
        handed.append(copy)
    mix_in[:, columns] = mix_out[pl.ds(pl.multiple_of(s * 8, 8), 8)]
    for copy in handed:
        copy.wait_recv()
    for q in range(4):
        own = slice(q * 1792, (q + 1) * 1792)
        out[:, own] = (rows[q] + mix_in[:, own]).astype(jnp.bfloat16)

    for copy in handed + tables + [swap] + moved:
        copy.wait_send()
    for k in range(4):
        for dz in range(4):
            if k or dz:
                dispatch(0, k, dz).wait_send()
                dispatch(1, k, dz).wait_send()
                give_back(k, dz).wait_send()
        for kind in range(6):
            gather(k, kind).wait_send()
        for kind in range(7):
            share(k, kind).wait_send()
    for copy in sent + first + second:
        copy.wait_send()
    each_far(lambda copy: copy.wait_send() if copy.is_remote else None)
    for half in (0, 1):
        for group in range(5):
            for kind in range(4 if group == 4 else 2):
                gather_copy(half, group if group < 4 else None, kind, (y, z)).wait_send()


def layer_call(*arrays):
    vmem = pl.BlockSpec(memory_space=pltpu.VMEM)
    anywhere = pl.BlockSpec(memory_space=pl.ANY)
    bf16, f32 = jnp.bfloat16, jnp.float32
    dma = pltpu.SemaphoreType.DMA
    return pl.pallas_call(
        layer_kernel,
        name="layer",
        out_shape=jax.ShapeDtypeStruct((8, 7168), bf16),
        in_specs=[anywhere, anywhere, vmem, vmem, vmem, anywhere, vmem, vmem, vmem, anywhere, anywhere, anywhere],
        out_specs=vmem,
        scratch_shapes=[
            pltpu.VMEM((4, 8, 576, 128), bf16),
            pltpu.VMEM((512, 576), bf16),
            pltpu.VMEM((4, 2, 128, 512), f32),
            pltpu.VMEM((512, 128), f32),
            pltpu.VMEM((512, 128), f32),
            pltpu.VMEM((512, 512), f32),
            pltpu.VMEM((128, 512), bf16),
            pltpu.VMEM((512, 7168), bf16),
            pltpu.VMEM((2, 16, 16, 1792), bf16),
            pltpu.VMEM((2, 3, 4, 16, 1792), bf16),
            pltpu.VMEM((2, 4, 16, 1792), bf16),
            pltpu.VMEM((2, 3, 16, 1792), bf16),
            pltpu.VMEM((4, 8, 1792), f32),
            pltpu.VMEM((8, 64, 128), f32),
            pltpu.VMEM((2, 64, 512), bf16),
            pltpu.VMEM((2, 256, 32), bf16),
            pltpu.VMEM((2, 32, 1792), bf16),
            pltpu.VMEM((2, 16, 16, 1792), bf16),
            pltpu.VMEM((2, 16, 16, 1792), bf16),
            pltpu.VMEM((4, 128, 7168), bf16),
            pltpu.VMEM((7168, 512), bf16),
            pltpu.VMEM((2048, 896), bf16),
            pltpu.VMEM((128, 512), f32),
            pltpu.VMEM((4, 128, 2048), bf16),
            pltpu.VMEM((4, 4, 32, 896), bf16),
            pltpu.VMEM((16, 32, 896), bf16),
            pltpu.VMEM((64, 896), f32),
            pltpu.VMEM((8, 7168), f32),
            dma((2, 7)), dma((2, 7)),
            dma((2, 5, 4)), dma((2, 5, 4)),
            dma((2, 2, 3)), dma((2, 2, 3)),
            dma((7,)), dma((7,)),
            dma((6,)),
            dma((8,)), dma((8,)),
            dma((2, 4, 4)), dma((2, 4, 4)),
            dma((4, 6)), dma((4, 6)),
            dma((4, 7)), dma((4, 7)),
            dma((4, 4)), dma((4, 4)),
            dma((7,)), dma((7,)),
        ],
        compiler_params=pltpu.CompilerParams(
            collective_id=0, has_side_effects=True, vmem_limit_bytes=60 << 20
        ),
    )(*arrays)


def serve_kernel(group_passages, passage_place, latents, served, served_far, sem):
    s, e = lax.axis_index("store"), lax.axis_index("ep")
    y, z = e // 4, e % 4
    copies = []
    for g in range(8):
        def piece(j, q, dst, i):
            place = passage_place[group_passages[g * 32 + s * 4 + j]] - s * 32
            copy = pltpu.make_async_copy(
                latents.at[place, pl.ds(pl.multiple_of(q * 144, 16), 144)], dst, sem.at[g, i]
            )
            copy.start()
            copies.append(copy)

        piece(y, z, served.at[g], 4)
        for i in range(4):
            piece(
                jnp.where(s < 4, i, lax.rem(y + 2, 4)), jnp.where(s < 4, lax.rem(z + 2, 4), i),
                served_far.at[g, i], i,
            )
    for copy in copies:
        copy.wait()


def serve(latent_store, group_passages, passage_place):
    smem = pl.BlockSpec(memory_space=pltpu.SMEM)
    vmem = pl.BlockSpec(memory_space=pltpu.VMEM)
    anywhere = pl.BlockSpec(memory_space=pl.ANY)
    return pl.pallas_call(
        serve_kernel,
        name="serve",
        out_shape=(
            jax.ShapeDtypeStruct((8, 144, 128), jnp.bfloat16),
            jax.ShapeDtypeStruct((8, 4, 144, 128), jnp.bfloat16),
        ),
        in_specs=[smem, smem, anywhere],
        out_specs=(vmem, vmem),
        scratch_shapes=[pltpu.SemaphoreType.DMA((8, 5))],
    )(group_passages, passage_place, jnp.swapaxes(latent_store, 1, 2))


def body(
    queries, residual_in, latent_store, group_passages, row_slots, passage_place, w_uv, w_out,
    expert_ids, expert_gates, w_gate, w_up, w_down,
):
    served, served_far = serve(latent_store, group_passages, passage_place)
    return layer_call(
        served, served_far, queries, row_slots.T, w_uv, w_out, residual_in,
        expert_ids.T, expert_gates.T, w_gate[0], w_up[0], w_down[0],
    )


def solution(mesh):
    return jax.shard_map(
        body,
        mesh=mesh,
        in_specs=(
            P("store", "ep"),
            P(("store", "ep"), None),
            P("store", None, None),
            P(),
            P("store", None),
            P(),
            P("ep", None, None),
            P("ep", None),
            P(("store", "ep"), None),
            P(("store", "ep"), None),
            P("ep", None, "store"),
            P("ep", None, "store"),
            P("ep", "store", None),
        ),
        out_specs=P(("store", "ep"), None),
        check_vma=False,
    )
```

```python
import functools

import jax
import jax.numpy as jnp
from jax import lax
from jax.experimental import pallas as pl
from jax.experimental.pallas import tpu as pltpu
from jax.sharding import PartitionSpec as P

SCALE = 192.0 ** (-0.5) * 1.4426950408889634
MESH = pl.DeviceIdType.MESH
LOW = -1e29
FAR_LOW = 1e30


def offset_of(i):
    return i + i // 2 - 2 * (i // 3)


def layer_kernel(
    served, served_far, queries, row_slots, w_uv, w_out, residual, ids, gates, w_gate, w_up, w_down,
    out,
    kv, heads, mask, top, total, acc, head_out, out_w, part, part_in, summed, summed_in, rows,
    raw, weights, shrink, table, weigh, places, normed, outgoing, arrived, x_rows, in_w, down_w, pre, hid, y_part, returned, mix_out, mix_in,
    x_send, x_recv, g_send, g_recv, r_send, r_recv, d_send, d_recv, w_sem,
    n_send, n_recv, t_send, t_recv, a_send, a_recv, h_send, h_recv, b_send, b_recv, m_send, m_recv,
):
    s = lax.axis_index("store")
    e = lax.axis_index("ep")
    y, z = e // 4, e % 4

    def at_y(d):
        return (s, lax.rem(y + d, 4) * 4 + z)

    def at_z(d):
        return (s, y * 4 + lax.rem(z + d, 4))

    def at_s(d):
        return (lax.rem(s + d, 8), e)

    def quarter(q):
        return pl.ds(pl.multiple_of(q * 144, 16), 144)

    sibling = s + 1 - 2 * (s % 2)

    def on_ep(dy, dz):
        return lax.rem(y + dy, 4) * 4 + lax.rem(z + dz, 4)

    peers = [at_s(d) for d in range(1, 8)]
    peers += [(s, on_ep(dy, dz)) for dy in range(4) for dz in range(4) if dy or dz]
    barrier = pltpu.get_barrier_semaphore()
    for peer in peers:
        pl.semaphore_signal(barrier, inc=1, device_id=peer, device_id_type=MESH)
    get_w = pltpu.make_async_copy(w_out, out_w, w_sem.at[0])
    get_in = [
        pltpu.make_async_copy(w_gate, in_w.at[:, 0:256], w_sem.at[4]),
        pltpu.make_async_copy(w_up, in_w.at[:, 256:512], w_sem.at[5]),
    ]
    for load in [get_w] + get_in:
        load.start()

    lane_row = lax.broadcasted_iota(jnp.int32, (1, 128), 1) % 8
    repeat = (lax.broadcasted_iota(jnp.int32, (8, 1), 0) == lane_row).astype(jnp.float32)
    wide_ids = jnp.dot(ids[...].astype(jnp.float32), repeat, preferred_element_type=jnp.float32)
    wide_gates = jnp.dot(
        gates[...], repeat, preferred_element_type=jnp.float32, precision=lax.Precision.HIGHEST
    )
    pair = lax.broadcasted_iota(jnp.int32, (64, 1), 0)
    expert = (pair // 4).astype(jnp.float32)
    routed = jnp.zeros((64, 128), jnp.float32)
    gate = jnp.zeros((64, 128), jnp.float32)
    for i in range(4):
        named = (wide_ids[i:i + 1] == expert).astype(jnp.float32)
        routed = routed + named
        gate = gate + named * wide_gates[i:i + 1]
    before = lax.broadcasted_iota(jnp.int32, (128, 1), 0)
    upto = lax.broadcasted_iota(jnp.int32, (1, 128), 1) % 8
    earlier = jnp.dot(
        routed.astype(jnp.bfloat16), (before < upto).astype(jnp.bfloat16), preferred_element_type=jnp.float32
    )
    table[s] = jnp.where((routed > 0.5) & (earlier == (pair % 4).astype(jnp.float32)), gate, 0.0)
    pl.semaphore_wait(barrier, len(peers))

    sent = []
    for d in range(1, 8):
        to = at_s(d)
        copy = pltpu.make_async_remote_copy(
            src_ref=served.at[to[0]], dst_ref=kv.at[y, s, quarter(z)],
            send_sem=x_send.at[0, d - 1], recv_sem=x_recv.at[0, d - 1],
            device_id=to, device_id_type=MESH,
        )
        copy.start()
        sent.append(copy)
    keep = pltpu.make_async_copy(served.at[s], kv.at[y, s, quarter(z)], w_sem.at[2])
    keep.start()

    def copy_to(src, dst, send, recv, device):
        return pltpu.make_async_remote_copy(
            src_ref=src, dst_ref=dst, send_sem=send, recv_sem=recv, device_id=device, device_id_type=MESH
        )

    def far_copies(whole):
        def target(ref):
            return ref.at[lax.rem(y + 2, 4), s] if whole else ref.at[:, s, quarter(lax.rem(z + 2, 4))]

        def source(g):
            return served_far.at[g].reshape(576, 128) if whole else served_far.at[g]

        return [
            pltpu.make_async_remote_copy(
                src_ref=source(at_s(d)[0]), dst_ref=target(kv),
                send_sem=x_send.at[1, d - 1], recv_sem=x_recv.at[1, d - 1],
                device_id=at_s(d), device_id_type=MESH,
            )
            for d in range(1, 8)
        ] + [pltpu.make_async_copy(source(s), target(kv), w_sem.at[3])]

    def each_far(act):
        for whole in (False, True):
            @pl.when((s >= 4) if whole else (s < 4))
            def _():
                for copy in far_copies(whole):
                    act(copy)

    tables = []
    for d in range(1, 8):
        copy = pltpu.make_async_remote_copy(
            src_ref=table.at[s], dst_ref=table.at[s], send_sem=n_send.at[d], recv_sem=n_recv.at[d],
            device_id=at_s(d), device_id_type=MESH,
        )
        copy.start()
        tables.append(copy)
    each_far(lambda copy: copy.start())

    for h in range(4):
        heads[h * 128:(h + 1) * 128] = queries[:, h * 576:(h + 1) * 576]
    slot = lax.broadcasted_iota(jnp.int32, (32, 1), 0)
    chosen = jnp.zeros((32, 128), jnp.bool_)
    for i in range(16):
        chosen = chosen | (row_slots[i:i + 1] == slot)
    chosen = chosen.astype(jnp.bfloat16)
    slot_row = lax.broadcasted_iota(jnp.int32, (32, 1), 0)
    token_col = lax.broadcasted_iota(jnp.int32, (1, 512), 1)
    for j in range(4):
        for half in (0, 1):
            spread = (slot_row == (token_col // 128 + 4 * half) * 4 + j).astype(jnp.bfloat16)
            live = lax.dot_general(
                chosen, spread, (((0,), (0,)), ((), ())), preferred_element_type=jnp.float32
            )
            mask[j, half] = (live - 1.0) * FAR_LOW
    top[...] = jnp.full_like(top, LOW)
    total[...] = jnp.zeros_like(total)
    acc[...] = jnp.zeros_like(acc)

    def chunk(half, first, second):
        dy, dz = (first, second) if half == 0 else (second, first)
        return lax.rem(y - dy + 4, 4), lax.rem(z - dz + 4, 4)

    def attend(j, half):
        keys = jnp.concatenate([kv[j, half * 4 + i] for i in range(4)], axis=1)
        raw[...] = jnp.dot(heads[...], keys, preferred_element_type=jnp.float32)
        for low in range(0, 512, 64):
            own = slice(low, low + 64)
            scores = raw[own] * SCALE + mask[j, half, low % 128:low % 128 + 64]
            old = top[own]
            new = jnp.maximum(old, jnp.max(scores, axis=1, keepdims=True))
            exponent = jnp.exp2(scores - new[:, 0:1])
            scale = jnp.exp2(old - new)
            top[own] = new
            total[own] = total[own] * scale + jnp.sum(exponent, axis=1, keepdims=True)
            shrink[own] = scale
            weights[own] = exponent.astype(jnp.bfloat16)
        acc[...] = acc[...] * shrink[:, 0:1] + lax.dot_general(
            weights[...], keys[0:512], (((1,), (1,)), ((), ())), preferred_element_type=jnp.float32
        )

    def build_weigh():
        lane = lax.broadcasted_iota(jnp.int32, (1, 128), 1)
        gated = jnp.concatenate([jnp.where(lane // 8 == g, table[g], 0.0) for g in range(8)], axis=0)
        from_row = lax.broadcasted_iota(jnp.int32, (512, 1), 0)
        to_col = lax.broadcasted_iota(jnp.int32, (1, 512), 1)
        place = (to_col // 4 % 8) * 64 + (to_col // 32) * 4 + to_col % 4
        move = (from_row == place).astype(jnp.bfloat16)
        high = gated.astype(jnp.bfloat16)
        low = (gated - high.astype(jnp.float32)).astype(jnp.bfloat16)
        for i, held in ((0, high), (1, low)):
            weigh[i] = lax.dot_general(
                held, move, (((0,), (0,)), ((), ())), preferred_element_type=jnp.float32
            )[0:64].astype(jnp.bfloat16)

    def build_place(side):
        group = lax.rem(s + 4 * side, 8)
        to_row = lax.broadcasted_iota(jnp.int32, (256, 1), 0)
        from_pair = lax.broadcasted_iota(jnp.int32, (1, 64), 1)
        widen = (from_pair == (to_row // 16) * 4 + to_row % 4).astype(jnp.bfloat16)
        held = jnp.dot(
            widen, (table[group] > 0).astype(jnp.bfloat16), preferred_element_type=jnp.float32
        )[:, 0:32]
        row_quarter = lax.broadcasted_iota(jnp.int32, (256, 1), 0) // 4 % 4
        col_quarter = lax.broadcasted_iota(jnp.int32, (1, 32), 1) // 8
        places[side] = jnp.where(row_quarter == col_quarter, held, 0.0).astype(jnp.bfloat16)
    def gather_copy(half, group, kind, place):
        low = half * 4 + (2 if kind == 3 else 0)
        size = 2 if kind >= 2 else 4
        on_y = (half == 0) == (group is None)
        to = (at_y if on_y else at_z)(1 if kind % 2 == 0 else 3)
        block = kv.at[place[0], pl.ds(low, size), quarter(place[1])]
        index = 4 if group is None else group
        return pltpu.make_async_remote_copy(
            src_ref=block, dst_ref=block,
            send_sem=g_send.at[half, index, kind], recv_sem=g_recv.at[half, index, kind],
            device_id=to, device_id_type=MESH,
        )

    def launch(group, offset):
        for half in (0, 1):
            for kind in (0, 1):
                gather_copy(half, group, kind, chunk(half, offset, 0)).start()

    keep.wait()
    for copy in sent:
        copy.wait_recv()
    launch(None, 0)
    launch(0, 0)
    keep_w = pltpu.make_async_copy(
        w_down.at[:, pl.ds(pl.multiple_of(s * 896, 896), 896)],
        down_w.at[pl.ds(pl.multiple_of(s * 256, 256), 256)], w_sem.at[1],
    )
    keep_w.start()
    moved = []
    for d in range(1, 8):
        to = at_s(d)
        copy = pltpu.make_async_remote_copy(
            src_ref=w_down.at[:, pl.ds(pl.multiple_of(to[0] * 896, 896), 896)],
            dst_ref=down_w.at[pl.ds(pl.multiple_of(s * 256, 256), 256)],
            send_sem=d_send.at[d - 1], recv_sem=d_recv.at[d - 1],
            device_id=to, device_id_type=MESH,
        )
        if d != 4:
            copy.start()
        moved.append(copy)
    for kind in (0, 1):
        offset = 1 if kind == 0 else 3
        for half in (0, 1):
            gather_copy(half, None, kind, (y, z)).wait_recv()
            gather_copy(half, None, kind + 2, chunk(half, offset, 0)).start()
    launch(1, 1)
    launch(2, 3)
    for half in (0, 1):
        for kind in (2, 3):
            gather_copy(half, None, kind, (y, z)).wait_recv()
    launch(3, 2)
    attend(y, 1)

    def take_far(copy):
        if copy.is_remote:
            copy.wait_recv()
        else:
            copy.wait()

    each_far(take_far)
    attend(lax.rem(y + 2, 4), 1)

    def sides(i, _):
        for kind in (0, 1):
            for half in (0, 1):
                gather_copy(half, i, kind, (y, z)).wait_recv()
        attend(chunk(0, offset_of(i), 0)[0], 0)
        return 0

    lax.fori_loop(0, 4, sides, 0)

    def last(i, _):
        attend(lax.rem(y + 1 + 2 * i, 4), 1)
        return 0

    lax.fori_loop(0, 2, last, 0)

    for h in range(4):
        own = pl.ds(h * 128, 128)
        latent = (acc[own] / total[own, 0:1]).astype(jnp.bfloat16)
        head_out[:, h * 128:(h + 1) * 128] = jnp.dot(
            latent, w_uv[h], preferred_element_type=jnp.float32
        ).astype(jnp.bfloat16)
    get_w.wait()

    first = []
    for half in (0, 1):
        def project(t, _):
            lane = pl.multiple_of(t * 256, 256)
            both = []
            for k in (0, 1):
                column = pl.multiple_of(half * 3584 + k * 1792 + t * 256, 256)
                both.append(jnp.dot(
                    head_out[...], out_w[:, pl.ds(column, 256)], preferred_element_type=jnp.float32
                ).reshape(16, 8, 256))
            tile = jnp.concatenate(both, axis=1).astype(jnp.bfloat16)
            if half == 0:
                part[0, :, :, pl.ds(lane, 256)] = tile
            else:
                for p in range(16):
                    part[1, (p % 4) * 4 + p // 4, :, pl.ds(lane, 256)] = tile[p]
            return 0

        lax.fori_loop(0, 7, project, 0)
        for d in (1, 2, 3):
            to, line = (at_y(d), lax.rem(y + d, 4)) if half == 0 else (at_z(d), lax.rem(z + d, 4))
            copy = pltpu.make_async_remote_copy(
                src_ref=part.at[half, pl.ds(line * 4, 4)], dst_ref=part_in.at[half, d - 1],
                send_sem=r_send.at[half, 0, d - 1], recv_sem=r_recv.at[half, 0, d - 1],
                device_id=to, device_id_type=MESH,
            )
            copy.start()
            first.append(copy)
    for copy in tables:
        copy.wait_recv()
    build_place(0)
    build_place(1)
    second = []
    for half in (0, 1):
        for d in (1, 2, 3):
            first[half * 3 + d - 1].wait_recv()
        own = y if half == 0 else z

        def add(k, _):
            value = part[half, own * 4 + k].astype(jnp.float32)
            for d in range(3):
                value = value + part_in[half, d, k].astype(jnp.float32)
            summed[half, k] = value.astype(jnp.bfloat16)
            return 0

        lax.fori_loop(0, 4, add, 0)
        for d in (1, 2, 3):
            to, line = (at_z(d), lax.rem(z + d, 4)) if half == 0 else (at_y(d), lax.rem(y + d, 4))
            copy = pltpu.make_async_remote_copy(
                src_ref=summed.at[half, line], dst_ref=summed_in.at[half, d - 1],
                send_sem=r_send.at[half, 1, d - 1], recv_sem=r_recv.at[half, 1, d - 1],
                device_id=to, device_id_type=MESH,
            )
            copy.start()
            second.append(copy)
    squares = jnp.zeros((8, 1), jnp.float32)
    for half in (0, 1):
        for d in (1, 2, 3):
            second[half * 3 + d - 1].wait_recv()
        value = summed[half, z if half == 0 else y].astype(jnp.float32)
        for d in range(3):
            value = value + summed_in[half, d].astype(jnp.float32)
        for k in (0, 1):
            q = 2 * half + k
            row = residual[:, q * 1792:(q + 1) * 1792].astype(jnp.float32) + value[k * 8:(k + 1) * 8]
            rows[q] = row
            squares = squares + jnp.sum(row * row, axis=1, keepdims=True)
    norm = lax.rsqrt(squares / 7168.0 + 1e-06)
    for q in (0, 2):
        two = jnp.concatenate([rows[q] * norm, rows[q + 1] * norm], axis=0)
        normed[0, q * 8:(q + 2) * 8] = two.astype(jnp.bfloat16)

    swap = copy_to(normed.at[0], normed.at[1], n_send.at[0], n_recv.at[0], at_s(4))
    swap.start()
    moved[3].start()

    def dispatch(side, k, dz):
        to = on_ep(offset_of(k) + dz, dz)
        return copy_to(
            outgoing.at[side, to], arrived.at[side, e], t_send.at[side, k, dz], t_recv.at[side, k, dz], (s, to)
        )

    def give_back(k, dz):
        to = on_ep(4 - offset_of(k) + dz, dz)
        return copy_to(y_part.at[k, lax.rem(z + dz, 4)], returned.at[e], b_send.at[k, dz], b_recv.at[k, dz], (s, to))

    def gather(k, kind):
        to = at_s((2, 6)[kind]) if kind < 2 else (sibling, e)
        block = lax.rem(s + (0, 0, 0, 4, 6, 2)[kind], 8)
        ref = x_rows.at[k, pl.ds(pl.multiple_of(block * 16, 16), 16)]
        return copy_to(ref, ref, a_send.at[k, kind], a_recv.at[k, kind], to)

    def share(k, kind):
        to = at_s((2, 6, 4)[kind]) if kind < 3 else (sibling, e)
        block = lax.rem(s + (0, 0, 0, 0, 6, 2, 4)[kind], 8)
        ref = hid.at[k, :, pl.ds(pl.multiple_of(block * 256, 256), 256)]
        return copy_to(ref, ref, h_send.at[k, kind], h_recv.at[k, kind], to)

    def spread_rows(side):
        outgoing[side] = jnp.dot(
            places[side], normed[side], preferred_element_type=jnp.float32
        ).astype(jnp.bfloat16).reshape(16, 16, 1792)
        arrived[side, e] = outgoing[side, e]

    def send_rows(side, k, own=False):
        for dz in (2, 1, 3) if own else (2, 1, 3, 0):
            dispatch(side, k, dz).start()

    spread_rows(0)
    send_rows(0, 0, True)
    send_rows(0, 1)
    swap.wait_recv()
    spread_rows(1)
    send_rows(1, 0, True)
    for side, k in ((0, 2), (1, 1), (0, 3), (1, 2), (1, 3)):
        send_rows(side, k)

    rows16 = lax.broadcasted_iota(jnp.int32, (16, 1), 0)
    cols64 = lax.broadcasted_iota(jnp.int32, (1, 64), 1)

    def enter(side, k):
        for dz in range(1, 4):
            dispatch(side, k, dz).wait_recv()

        @pl.when(k > 0)
        def _():
            dispatch(side, k, 0).wait_recv()

        block = jnp.concatenate([
            arrived[side, lax.rem(y - z + 8 - offset_of(k) + i, 4) * 4 + i] for i in range(4)
        ], axis=0)
        low = pl.multiple_of(lax.rem(s + 4 * side, 8) * 16, 16)
        for q in range(4):
            take = (cols64 == (rows16 // 4) * 16 + q * 4 + rows16 % 4).astype(jnp.bfloat16)
            x_rows[k, pl.ds(low, 16), q * 1792:(q + 1) * 1792] = jnp.dot(
                take, block, preferred_element_type=jnp.float32
            ).astype(jnp.bfloat16)
        for kind in ((0, 1, 2), (3,))[side]:
            gather(k, kind).start()

    def pass_on(k):
        for kind in (0, 1):
            gather(k, kind).wait_recv()
            gather(k, kind + 4).start()

    def hidden(k):
        for kind in range(2, 6):
            gather(k, kind).wait_recv()
        pre[...] = jnp.zeros_like(pre)

        def add(q, _):
            low = pl.multiple_of(q * 1792, 1792)
            pre[...] += jnp.dot(
                x_rows[k, :, pl.ds(low, 1792)], in_w[pl.ds(low, 1792)], preferred_element_type=jnp.float32
            )
            return 0

        lax.fori_loop(0, 4, add, 0)
        gate = pre[:, 0:256]
        hid[k, :, pl.ds(pl.multiple_of(s * 256, 256), 256)] = (
            gate / (1.0 + jnp.exp(-gate)) * pre[:, 256:512]
        ).astype(jnp.bfloat16)
        for kind in range(4):
            share(k, kind).start()

    to128 = lax.broadcasted_iota(jnp.int32, (128, 1), 0)
    from128 = lax.broadcasted_iota(jnp.int32, (1, 128), 1)

    def project(k):
        for kind in range(3):
            share(k, kind).wait_recv()
            share(k, kind + 4).start()
        for kind in range(3, 7):
            share(k, kind).wait_recv()
        value = jnp.dot(hid[k], down_w[...], preferred_element_type=jnp.float32).astype(jnp.bfloat16)
        order = (from128 == (to128 // 4 % 8) * 16 + (to128 // 32) * 4 + to128 % 4).astype(jnp.bfloat16)
        y_part[k] = jnp.dot(order, value, preferred_element_type=jnp.float32).astype(jnp.bfloat16).reshape(4, 32, 896)
        for dz in range(1, 4):
            give_back(k, dz).start()

        @pl.when(k > 0)
        def _():
            give_back(k, 0).start()

        @pl.when(k == 0)
        def _():
            returned[e] = y_part[k, z]

    def step(t, _):
        @pl.when(t < 4)
        def _():
            enter(0, t)

        @pl.when(t == 0)
        def _():
            build_weigh()

        @pl.when(t == 1)
        def _():
            for load in get_in:
                load.wait()

        @pl.when((t >= 1) & (t < 5))
        def _():
            enter(1, t - 1)
            pass_on(t - 1)
            hidden(t - 1)

        @pl.when(t == 2)
        def _():
            keep_w.wait()
            for copy in moved:
                copy.wait_recv()

        @pl.when(t >= 2)
        def _():
            project(t - 2)

        return 0

    lax.fori_loop(0, 6, step, 0)

    for k in range(4):
        for dz in range(4):
            if k or dz:
                give_back(k, dz).wait_recv()
    back = returned[...].reshape(512, 896)
    mix_out[...] = jnp.dot(weigh[0], back, preferred_element_type=jnp.float32) + jnp.dot(
        weigh[1], back, preferred_element_type=jnp.float32
    )
    columns = pl.ds(pl.multiple_of(s * 896, 896), 896)
    handed = []
    for d in (4, 2, 6, 3, 5, 1, 7):
        to = at_s(d)
        copy = copy_to(
            mix_out.at[pl.ds(pl.multiple_of(to[0] * 8, 8), 8)], mix_in.at[:, columns],
            m_send.at[d - 1], m_recv.at[d - 1], to,
        )
        copy.start()
        handed.append(copy)
    mix_in[:, columns] = mix_out[pl.ds(pl.multiple_of(s * 8, 8), 8)]
    for copy in handed:
        copy.wait_recv()
    for q in range(4):
        own = slice(q * 1792, (q + 1) * 1792)
        out[:, own] = (rows[q] + mix_in[:, own]).astype(jnp.bfloat16)

    for copy in handed + tables + [swap] + moved:
        copy.wait_send()
    for k in range(4):
        for dz in range(4):
            if k or dz:
                dispatch(0, k, dz).wait_send()
                dispatch(1, k, dz).wait_send()
                give_back(k, dz).wait_send()
        for kind in range(6):
            gather(k, kind).wait_send()
        for kind in range(7):
            share(k, kind).wait_send()
    for copy in sent + first + second:
        copy.wait_send()
    each_far(lambda copy: copy.wait_send() if copy.is_remote else None)
    for half in (0, 1):
        for group in range(5):
            for kind in range(4 if group == 4 else 2):
                gather_copy(half, group if group < 4 else None, kind, (y, z)).wait_send()


def layer_call(*arrays):
    vmem = pl.BlockSpec(memory_space=pltpu.VMEM)
    anywhere = pl.BlockSpec(memory_space=pl.ANY)
    bf16, f32 = jnp.bfloat16, jnp.float32
    dma = pltpu.SemaphoreType.DMA
    return pl.pallas_call(
        layer_kernel,
        name="layer",
        out_shape=jax.ShapeDtypeStruct((8, 7168), bf16),
        in_specs=[anywhere, anywhere, vmem, vmem, vmem, anywhere, vmem, vmem, vmem, anywhere, anywhere, anywhere],
        out_specs=vmem,
        scratch_shapes=[
            pltpu.VMEM((4, 8, 576, 128), bf16),
            pltpu.VMEM((512, 576), bf16),
            pltpu.VMEM((4, 2, 128, 512), f32),
            pltpu.VMEM((512, 128), f32),
            pltpu.VMEM((512, 128), f32),
            pltpu.VMEM((512, 512), f32),
            pltpu.VMEM((128, 512), bf16),
            pltpu.VMEM((512, 7168), bf16),
            pltpu.VMEM((2, 16, 16, 1792), bf16),
            pltpu.VMEM((2, 3, 4, 16, 1792), bf16),
            pltpu.VMEM((2, 4, 16, 1792), bf16),
            pltpu.VMEM((2, 3, 16, 1792), bf16),
            pltpu.VMEM((4, 8, 1792), f32),
            pltpu.VMEM((512, 512), f32),
            pltpu.VMEM((512, 512), bf16),
            pltpu.VMEM((512, 128), f32),
            pltpu.VMEM((8, 64, 128), f32),
            pltpu.VMEM((2, 64, 512), bf16),
            pltpu.VMEM((2, 256, 32), bf16),
            pltpu.VMEM((2, 32, 1792), bf16),
            pltpu.VMEM((2, 16, 16, 1792), bf16),
            pltpu.VMEM((2, 16, 16, 1792), bf16),
            pltpu.VMEM((4, 128, 7168), bf16),
            pltpu.VMEM((7168, 512), bf16),
            pltpu.VMEM((2048, 896), bf16),
            pltpu.VMEM((128, 512), f32),
            pltpu.VMEM((4, 128, 2048), bf16),
            pltpu.VMEM((4, 4, 32, 896), bf16),
            pltpu.VMEM((16, 32, 896), bf16),
            pltpu.VMEM((64, 896), f32),
            pltpu.VMEM((8, 7168), f32),
            dma((2, 7)), dma((2, 7)),
            dma((2, 5, 4)), dma((2, 5, 4)),
            dma((2, 2, 3)), dma((2, 2, 3)),
            dma((7,)), dma((7,)),
            dma((6,)),
            dma((8,)), dma((8,)),
            dma((2, 4, 4)), dma((2, 4, 4)),
            dma((4, 6)), dma((4, 6)),
            dma((4, 7)), dma((4, 7)),
            dma((4, 4)), dma((4, 4)),
            dma((7,)), dma((7,)),
        ],
        compiler_params=pltpu.CompilerParams(
            collective_id=0, has_side_effects=True, vmem_limit_bytes=60 << 20
        ),
    )(*arrays)


def serve_kernel(group_passages, passage_place, latents, served, served_far, sem):
    s, e = lax.axis_index("store"), lax.axis_index("ep")
    y, z = e // 4, e % 4
    copies = []
    for g in range(8):
        def piece(j, q, dst, i):
            place = passage_place[group_passages[g * 32 + s * 4 + j]] - s * 32
            copy = pltpu.make_async_copy(
                latents.at[place, pl.ds(pl.multiple_of(q * 144, 16), 144)], dst, sem.at[g, i]
            )
            copy.start()
            copies.append(copy)

        piece(y, z, served.at[g], 4)
        for i in range(4):
            piece(
                jnp.where(s < 4, i, lax.rem(y + 2, 4)), jnp.where(s < 4, lax.rem(z + 2, 4), i),
                served_far.at[g, i], i,
            )
    for copy in copies:
        copy.wait()


def serve(latent_store, group_passages, passage_place):
    smem = pl.BlockSpec(memory_space=pltpu.SMEM)
    vmem = pl.BlockSpec(memory_space=pltpu.VMEM)
    anywhere = pl.BlockSpec(memory_space=pl.ANY)
    return pl.pallas_call(
        serve_kernel,
        name="serve",
        out_shape=(
            jax.ShapeDtypeStruct((8, 144, 128), jnp.bfloat16),
            jax.ShapeDtypeStruct((8, 4, 144, 128), jnp.bfloat16),
        ),
        in_specs=[smem, smem, anywhere],
        out_specs=(vmem, vmem),
        scratch_shapes=[pltpu.SemaphoreType.DMA((8, 5))],
    )(group_passages, passage_place, jnp.swapaxes(latent_store, 1, 2))


def body(
    queries, residual_in, latent_store, group_passages, row_slots, passage_place, w_uv, w_out,
    expert_ids, expert_gates, w_gate, w_up, w_down,
):
    served, served_far = serve(latent_store, group_passages, passage_place)
    return layer_call(
        served, served_far, queries, row_slots.T, w_uv, w_out, residual_in,
        expert_ids.T, expert_gates.T, w_gate[0], w_up[0], w_down[0],
    )


def solution(mesh):
    return jax.shard_map(
        body,
        mesh=mesh,
        in_specs=(
            P("store", "ep"),
            P(("store", "ep"), None),
            P("store", None, None),
            P(),
            P("store", None),
            P(),
            P("ep", None, None),
            P("ep", None),
            P(("store", "ep"), None),
            P(("store", "ep"), None),
            P("ep", None, "store"),
            P("ep", None, "store"),
            P("ep", "store", None),
        ),
        out_specs=P(("store", "ep"), None),
        check_vma=False,
    )
```
